128 devices in a mesh: gx: 4 (over z), gy: 32 (over y, x, core).
Axes of the slice: x: 4, y: 4, z: 4, core: 2. Of those that a mesh axis runs over, the one named last changes fastest.
Arguments:
- heat_source: float32 [6144, 1024], P(('gx', 'gy')), may hold values from -18 to 18
- stiffness: float32 [2048, 384, 384], P(('gx', 'gy')), may hold values from -1 to 32, as said below
- element_faces: int32 [2048, 6], P(('gx', 'gy')), may hold values from 0 to 6143, as said below
Outputs:
- solution: float32 [6144, 1024], P(('gx', 'gy'))
- residual: float32 [6144, 1024], P(('gx', 'gy'))
The draws below stay inside these ranges and needn't reach their ends.
Inputs may be any that keep to these rules, and one draw needn't show every extreme that they name: `element_faces`: the elements form a periodic grid of 8 x 64 x 4 hexahedra; device (i, j) of gx and gy holds the block of 2 x 2 x 4 elements at streamwise block i and spanwise block j, in a local order of its own, and owns the lower x, lower y and lower z faces of its elements, numbered in an order of its own. So every face number appears exactly twice, and a device's elements reference faces of itself, of the next device along gx (cyclic, same gy index; exactly 8 references) and of the next device along gy (cyclic, same gx index; exactly 8 references). `stiffness`: each element matrix is symmetric with a positive diagonal and strictly diagonally dominant.
All inputs are finite; a program needn't handle non-finite values.
Results may differ from the reference program's by a relative error of at most 0.0002.
Values sent between devices are 32-bit elements; how exact they have to be, the bound alone decides.
No kernel may reach another device: no remote copies, remote signals or barrier semaphores. Data moves between devices by JAX's collectives and lax.ppermute only.
A program may use at most 128 MiB of HBM per device.

```python
import math
import jax
import jax.numpy as jnp
from jax import lax

BLOCK = 64
EX = 2
EY = 2
EZ = 4
SOURCES = 16
ITERS = 3
E_DEV = 16
FACE_DEV = 48
SPAN_X = 8
SPAN_Y = 64
ELEMENTS = 2048
FACES = 6144


def draw_heat_source(key, part):
    device_count = FACES // FACE_DEV
    row_device = (jnp.arange(FACES) // FACE_DEV).astype(jnp.float32)
    device_ramp = (1.0 + 2.0 * row_device / max(device_count - 1, 1))[:, None]
    base_draw = jax.random.truncated_normal(key, -6.0, 6.0, (FACES, SOURCES * BLOCK), jnp.float32)
    return base_draw * device_ramp


def draw_stiffness(key, part):
    block_order = 6 * BLOCK
    identity = jnp.eye(block_order, dtype=jnp.float32)
    diag_high = 2.0
    scale_high = math.log(8.0)

    def draw_element(element_index):
        sub_key = jax.random.fold_in(key, element_index)
        key_off = jax.random.fold_in(sub_key, 1)
        key_diag = jax.random.fold_in(sub_key, 2)
        key_scale = jax.random.fold_in(sub_key, 3)
        weights = jax.random.uniform(key_off, (block_order, block_order), jnp.float32, -1.0, 3.0)
        weights = 0.5 * (weights + weights.T)
        diagonal = jax.random.uniform(key_diag, (block_order, 1), jnp.float32, 1.0, diag_high)
        element_scale = jnp.exp(jax.random.uniform(key_scale, (), jnp.float32, 0.0, scale_high))
        return element_scale * (identity * diagonal + (1.0 - identity) * (-0.3 / block_order) * weights)
    return lax.map(draw_element, jnp.arange(ELEMENTS))


def draw_element_faces(key, part):
    device_count = ELEMENTS // E_DEV
    inner = SPAN_Y // EY
    cell_keys = jax.random.split(jax.random.fold_in(key, 21), device_count)
    face_keys = jax.random.split(jax.random.fold_in(key, 22), device_count)
    cell_orders = jax.vmap(lambda sub_key: jax.random.permutation(sub_key, E_DEV))(cell_keys).astype(jnp.int32)
    face_orders = jax.vmap(lambda sub_key: jax.random.permutation(sub_key, 3 * E_DEV))(face_keys).astype(jnp.int32)
    element_ids = jnp.arange(ELEMENTS, dtype=jnp.int32)
    device_ids = element_ids // E_DEV
    cell = cell_orders[device_ids, element_ids % E_DEV]
    local_x = cell // (EY * EZ)
    local_y = cell // EZ % EY
    local_z = cell % EZ
    place_x = device_ids // inner * EX + local_x
    place_y = device_ids % inner * EY + local_y

    def face_of(spot_x, spot_y, spot_z, kind):
        spot_x = spot_x % SPAN_X
        spot_y = spot_y % SPAN_Y
        spot_z = spot_z % EZ
        owner = spot_x // EX * inner + spot_y // EY
        owner_cell = (spot_x % EX * EY + spot_y % EY) * EZ + spot_z
        return owner * FACE_DEV + face_orders[owner, owner_cell * 3 + kind]
    columns = [face_of(place_x, place_y, local_z, 0), face_of(place_x + 1, place_y, local_z, 0), face_of(place_x, place_y, local_z, 1), face_of(place_x, place_y + 1, local_z, 1), face_of(place_x, place_y, local_z, 2), face_of(place_x, place_y, local_z + 1, 2)]
    return jnp.stack(columns, axis=1).astype(jnp.int32)


def setup_inputs(seed: int = 0) -> dict:
    key_of = jax.random.split(jax.random.key(seed), 4)
    heat_source = draw_heat_source(jax.random.fold_in(key_of[3], 71), 0)
    stiffness = draw_stiffness(jax.random.fold_in(key_of[3], 71), 0)
    element_faces = draw_element_faces(jax.random.fold_in(key_of[3], 71), 0)
    return dict(heat_source=heat_source, stiffness=stiffness, element_faces=element_faces)


def operate(vector, stiffness, element_faces):
    face_count = vector.shape[0]
    flat_faces = element_faces.reshape(-1).astype(jnp.int32)
    blocks = vector[flat_faces].reshape(ELEMENTS, 6, SOURCES, BLOCK)
    matrix = stiffness.reshape(ELEMENTS, 6, BLOCK, 6, BLOCK)
    flux_terms = jnp.einsum("ekbjc,ejsc->eksb", matrix, blocks, precision=lax.Precision.HIGHEST, preferred_element_type=jnp.float32)
    return jax.ops.segment_sum(flux_terms.reshape(ELEMENTS * 6, SOURCES * BLOCK), flat_faces, num_segments=face_count)


def source_sum(first_vec, second_vec):
    return jnp.sum((first_vec * second_vec).reshape(-1, SOURCES, BLOCK), axis=(0, 2))


def spread(per_source):
    return jnp.repeat(per_source, BLOCK)[None, :]


def reference(heat_source, stiffness, element_faces):
    solution = jnp.zeros_like(heat_source)
    residual = heat_source
    direction = heat_source
    norm_now = source_sum(residual, residual)
    for iteration in range(ITERS):
        applied = operate(direction, stiffness, element_faces)
        step_size = norm_now / source_sum(direction, applied)
        solution = solution + spread(step_size) * direction
        residual = residual - spread(step_size) * applied
        norm_next = source_sum(residual, residual)
        direction = residual + spread(norm_next / norm_now) * direction
        norm_now = norm_next
    return solution, residual
```

```python
import functools

import jax
import jax.numpy as jnp
from jax import lax
from jax.experimental import pallas as pl
from jax.experimental.pallas import tpu as pltpu
from jax.sharding import PartitionSpec as P

BLOCK = 64
SOURCES = 16
ELEMENTS = 16
ROWS = 48
SLOTS = 8
ORDER = 384

LOW = 0
UPP = 64
ROW_LOW = 128
ROW_UPP = 192
SEND_UP = 256
SEND_DOWN = 272
SEND_ROW = 288
SPARE = 304
TABLE = 312

VMEM = pl.BlockSpec(memory_space=pltpu.VMEM)
SMEM = pl.BlockSpec(memory_space=pltpu.SMEM)


def params():
    return pltpu.CompilerParams(vmem_limit_bytes=24 << 20)


def vmem(shape, dtype=jnp.float32):
    return pltpu.VMEM(shape, dtype)


def in_low_half(shape):
    return lax.broadcasted_iota(jnp.int32, shape, len(shape) - 1) < BLOCK


def table_kernel(ids, faces, source, table, down_x, down_y, owner, user):
    for row in range(ROWS):
        for part in range(3):
            user[part * ROWS + row] = -1
    own = ids[0]
    for element in range(ELEMENTS):
        for axis in range(3):
            row = faces[2 * axis, element] - own
            owner[row] = element * 4 + axis
            table[ROW_LOW + element * 4 + axis] = row
            row = faces[2 * axis + 1, element] - own
            if axis < 2:
                away = faces[2 * axis + 1, element] - ids[1 + axis] + ROWS * (1 + axis)
                here = jnp.logical_and(row >= 0, row < ROWS)
                user[jnp.where(here, row, away)] = element
            else:
                user[row] = element
            table[ROW_UPP + element * 4 + axis] = row
    count = [jnp.int32(0), jnp.int32(0)]
    for row in range(ROWS):
        ref = owner[row]
        axis = ref & 3
        element = ref >> 2
        other = user[row]
        here = other >= 0
        slot = jnp.where(axis == 0, count[0], count[1])
        table[LOW + ref] = jnp.where(here, other, ELEMENTS + slot)
        table[jnp.where(here, UPP + other * 4 + axis, SPARE)] = element
        table[jnp.where(here, SPARE, SEND_DOWN + axis * SLOTS + slot)] = element
        table[jnp.where(here, SPARE, SEND_ROW + axis * SLOTS + slot)] = row
        step = jnp.where(here, 0, 1)
        count[0] = count[0] + jnp.where(axis == 0, step, 0)
        count[1] = count[1] + jnp.where(axis == 1, step, 0)
    for axis in range(2):
        slot = jnp.int32(0)
        for row in range(ROWS):
            element = user[ROWS * (1 + axis) + row]
            here = element >= 0
            at = element * 4 + axis
            table[jnp.where(here, UPP + at, SPARE)] = ELEMENTS + slot
            table[jnp.where(here, ROW_UPP + at, SPARE)] = ROWS + axis * SLOTS + slot
            table[jnp.where(here, SEND_UP + axis * SLOTS + slot, SPARE)] = element
            slot = slot + jnp.where(here, 1, 0)
    for axis, out in enumerate((down_x, down_y)):
        for slot in range(4):
            at = SEND_ROW + axis * SLOTS + slot
            out[slot] = jnp.concatenate([source[table[at]], source[table[at + 4]]], axis=1)


def split_kernel(matrix, high, low):
    def body(element, _):
        full = matrix[element]
        top = full.astype(jnp.bfloat16)
        high[element] = top
        low[element] = (full - top.astype(jnp.float32)).astype(jnp.bfloat16)
        return 0

    lax.fori_loop(0, ELEMENTS, body, 0)


def multiply(table, get, high, low, vector, flux, ups, downs, moments, left):
    low_half = in_low_half((SOURCES, 128))
    norm = jnp.zeros((SOURCES, 128), jnp.float32)
    energy = jnp.zeros((SOURCES, 128), jnp.float32)
    for element in range(ELEMENTS):
        tiles = []
        for axis in range(3):
            tile = get(element, axis)
            tiles.append(tile)
            vector[element, axis] = tile
            norm = norm + tile * tile
            first = tile.astype(jnp.bfloat16)
            rest = tile - first.astype(jnp.float32)
            second = rest.astype(jnp.bfloat16)
            third = (rest - second.astype(jnp.float32)).astype(jnp.bfloat16)
            for part, value in enumerate((first, second, third)):
                left[element, part * 16 : part * 16 + 16, axis * 128 : axis * 128 + 128] = value
        rows = left[element]
        by_high = jnp.dot(rows, high[element], preferred_element_type=jnp.float32)
        by_low = jnp.dot(rows[:32], low[element], preferred_element_type=jnp.float32)
        total = by_high[0:16] + (by_high[16:32] + by_low[0:16] + (by_high[32:48] + by_low[16:32]))
        for axis in range(3):
            part = total[:, axis * 128 : axis * 128 + 128]
            flux[element, axis] = part
            energy = energy + tiles[axis] * part
    for axis in range(2):
        for slot in range(4):
            at = SEND_UP + axis * SLOTS + slot
            ups[axis][slot] = jnp.where(
                low_half, pltpu.roll(flux[table[at + 4], axis], 64, 1), flux[table[at], axis]
            )
            if downs is not None:
                at = SEND_DOWN + axis * SLOTS + slot
                downs[axis][slot] = jnp.where(
                    low_half, flux[table[at], axis], pltpu.roll(flux[table[at + 4], axis], 64, 1)
                )
    lane = lax.broadcasted_iota(jnp.int32, (SOURCES, 128), 1)
    half_norm = 0.5 * jnp.sum(norm, axis=1, keepdims=True)
    whole_energy = jnp.sum(energy, axis=1, keepdims=True)
    moments[...] = jnp.where(lane == 0, half_norm, jnp.where(lane == 1, whole_energy, 0.0))


def first_kernel(table, source, ghost_x, ghost_y, high, low,
                 vector, flux, up_x, up_y, down_x, down_y, moments, rows, left):
    for row in range(ROWS):
        rows[row] = source[row]
    for axis, ghost in enumerate((ghost_x, ghost_y)):
        for slot in range(4):
            rows[ROWS + axis * SLOTS + slot] = ghost[slot][:, :BLOCK]
            rows[ROWS + axis * SLOTS + slot + 4] = ghost[slot][:, BLOCK:]

    def get(element, axis):
        at = element * 4 + axis
        return jnp.concatenate([rows[table[ROW_LOW + at]], rows[table[ROW_UPP + at]]], axis=1)

    multiply(table, get, high, low, vector, flux, (up_x, up_y), (down_x, down_y), moments, left)


def gather_flux(previous, nexts, prevs, every):
    low_half = in_low_half((SOURCES, 128))
    every[0:ELEMENTS] = previous[...]
    for axis in range(2):
        for slot in range(4):
            ahead = nexts[axis][slot]
            behind = prevs[axis][slot]
            every[ELEMENTS + slot, axis] = jnp.where(low_half, ahead, behind)
            every[ELEMENTS + slot + 4, axis] = pltpu.roll(jnp.where(low_half, behind, ahead), 64, 1)


def later_kernel(last, table, previous, next_x, next_y, prev_x, prev_y, high, low,
                 vector, flux, up_x, up_y, *rest):
    if last:
        moments, every, left = rest
        downs = None
    else:
        down_x, down_y, moments, every, left = rest
        downs = (down_x, down_y)
    low_half = in_low_half((SOURCES, 128))
    gather_flux(previous, (next_x, next_y), (prev_x, prev_y), every)

    def get(element, axis):
        at = element * 4 + axis
        across = jnp.where(low_half, every[table[UPP + at], axis], every[table[LOW + at], axis])
        return every[element, axis] + pltpu.roll(across, 64, 1)

    multiply(table, get, high, low, vector, flux, (up_x, up_y), downs, moments, left)


def final_kernel(table, sums, zeroth, firsts, seconds, flux, prev_x, prev_y, answer, residual, every):
    mu = [sums[:, i : i + 1] for i in range(6)]
    centre_0 = mu[1] / mu[0]
    bent = {i: mu[i + 1] - centre_0 * mu[i] for i in range(1, 5)}
    centre_1 = bent[2] / bent[1] - centre_0
    span_1 = bent[1] / mu[0]
    twice = {i: bent[i + 1] - centre_1 * bent[i] - span_1 * mu[i] for i in (2, 3)}
    centre_2 = twice[3] / twice[2] - bent[2] / bent[1]
    span_2 = twice[2] / bent[1]
    alpha_0 = 1.0 / centre_0
    beta_0 = span_1 * alpha_0 * alpha_0
    alpha_1 = 1.0 / (centre_1 - span_1 * alpha_0)
    beta_1 = span_2 * alpha_1 * alpha_1
    alpha_2 = 1.0 / (centre_2 - span_2 * alpha_1)
    low_half = in_low_half((SOURCES, 128))
    every[0:ELEMENTS] = flux[...]
    for axis, prev in enumerate((prev_x, prev_y)):
        for slot in range(4):
            behind = prev[slot]
            every[ELEMENTS + slot, axis] = behind
            every[ELEMENTS + slot + 4, axis] = pltpu.roll(behind, 64, 1)
    for element in range(ELEMENTS):
        for axis in range(3):
            at = element * 4 + axis
            k0 = zeroth[element, axis]
            k1 = firsts[element, axis]
            k2 = seconds[element, axis]
            k3 = every[element, axis] + pltpu.roll(every[table[LOW + at], axis], 64, 1)
            r1 = k0 - alpha_0 * k1
            ar1 = k1 - alpha_0 * k2
            aar1 = k2 - alpha_0 * k3
            d1 = r1 + beta_0 * k0
            ad1 = ar1 + beta_0 * k1
            aad1 = aar1 + beta_0 * k2
            r2 = r1 - alpha_1 * ad1
            ar2 = ar1 - alpha_1 * aad1
            d2 = r2 + beta_1 * d1
            ad2 = ar2 + beta_1 * ad1
            x = alpha_0 * k0 + (alpha_1 * d1 + alpha_2 * d2)
            r = r2 - alpha_2 * ad2
            row = table[ROW_LOW + at]
            answer[row] = x[:, :BLOCK]
            residual[row] = r[:, :BLOCK]


def passed(value, axis, target):
    count = lax.axis_size(axis)
    return lax.ppermute(value, axis, [(i, target(i)) for i in range(count)])


def ahead(value, axis):
    return passed(value, axis, lambda i: (i + 1) % lax.axis_size(axis))


def back(value, axis):
    return passed(value, axis, lambda i: (i - 1) % lax.axis_size(axis))


def over_all(value):
    for step in (1, 2, 4, 8, 16):
        value = value + passed(value, "gy", lambda i: i ^ step)
    for step in (1, 2):
        value = value + passed(value, "gx", lambda i: i ^ step)
    return value


def local(heat_source, stiffness, element_faces):
    outer, inner = lax.axis_size("gx"), lax.axis_size("gy")
    at_x, at_y = lax.axis_index("gx"), lax.axis_index("gy")
    ids = jnp.stack(
        [
            at_x * inner + at_y,
            (at_x + 1) % outer * inner + at_y,
            at_x * inner + (at_y + 1) % inner,
        ]
    ).astype(jnp.int32) * ROWS
    source = heat_source.reshape(ROWS, SOURCES, BLOCK)
    pack = vmem((4, SOURCES, 128))
    state = vmem((ELEMENTS, 3, SOURCES, 128))
    matrix = vmem((ELEMENTS, ORDER, ORDER), jnp.bfloat16)
    moment = vmem((SOURCES, 128))
    left = pltpu.VMEM((ELEMENTS, 48, ORDER), jnp.bfloat16)
    every = pltpu.VMEM((ELEMENTS + SLOTS, 3, SOURCES, 128), jnp.float32)

    table, down_x, down_y = pl.pallas_call(
        table_kernel,
        out_shape=(jax.ShapeDtypeStruct((TABLE,), jnp.int32), pack, pack),
        in_specs=[SMEM, SMEM, VMEM],
        out_specs=(SMEM, VMEM, VMEM),
        scratch_shapes=[pltpu.SMEM((ROWS,), jnp.int32), pltpu.SMEM((3 * ROWS,), jnp.int32)],
        compiler_params=params(),
        name="table",
    )(ids, element_faces.T, source)
    ghost_x, ghost_y = back(down_x, "gx"), back(down_y, "gy")
    high, low = pl.pallas_call(
        split_kernel,
        out_shape=(matrix, matrix),
        in_specs=[VMEM],
        out_specs=(VMEM, VMEM),
        compiler_params=params(),
        cost_estimate=pl.CostEstimate(flops=10_000_000, bytes_accessed=18 << 20, transcendentals=0),
        name="split",
    )(stiffness)
    k0, flux, up_x, up_y, down_x, down_y, moment_0 = pl.pallas_call(
        first_kernel,
        out_shape=(state, state, pack, pack, pack, pack, moment),
        in_specs=[SMEM] + [VMEM] * 5,
        out_specs=(VMEM,) * 7,
        scratch_shapes=[pltpu.VMEM((64, SOURCES, BLOCK), jnp.float32), left],
        compiler_params=params(),
        name="first",
    )(table, source, ghost_x, ghost_y, high, low)

    def exchanged():
        return back(down_x, "gx"), back(down_y, "gy"), ahead(up_x, "gx"), ahead(up_y, "gy")

    next_x, next_y, prev_x, prev_y = exchanged()
    k1, flux, up_x, up_y, down_x, down_y, moment_1 = pl.pallas_call(
        functools.partial(later_kernel, False),
        out_shape=(state, state, pack, pack, pack, pack, moment),
        in_specs=[SMEM] + [VMEM] * 7,
        out_specs=(VMEM,) * 7,
        scratch_shapes=[every, left],
        compiler_params=params(),
        name="second",
    )(table, flux, next_x, next_y, prev_x, prev_y, high, low)
    next_x, next_y, prev_x, prev_y = exchanged()
    k2, flux, up_x, up_y, moment_2 = pl.pallas_call(
        functools.partial(later_kernel, True),
        out_shape=(state, state, pack, pack, moment),
        in_specs=[SMEM] + [VMEM] * 7,
        out_specs=(VMEM,) * 5,
        scratch_shapes=[every, left],
        compiler_params=params(),
        name="third",
    )(table, flux, next_x, next_y, prev_x, prev_y, high, low)
    sums = over_all(
        jnp.concatenate(
            [moment_0[:, :2], moment_1[:, :2], moment_2[:, :2], jnp.zeros((SOURCES, 122), jnp.float32)],
            axis=1,
        )
    )
    prev_x, prev_y = ahead(up_x, "gx"), ahead(up_y, "gy")
    answer, residual = pl.pallas_call(
        final_kernel,
        out_shape=(vmem((ROWS, SOURCES, BLOCK)),) * 2,
        in_specs=[SMEM] + [VMEM] * 7,
        out_specs=(VMEM, VMEM),
        scratch_shapes=[every],
        compiler_params=params(),
        name="final",
    )(table, sums, k0, k1, k2, flux, prev_x, prev_y)
    return answer.reshape(ROWS, SOURCES * BLOCK), residual.reshape(ROWS, SOURCES * BLOCK)


def solution(mesh):
    return jax.shard_map(
        local,
        mesh=mesh,
        in_specs=(P(("gx", "gy"), None), P(("gx", "gy"), None, None), P(("gx", "gy"), None)),
        out_specs=(P(("gx", "gy"), None), P(("gx", "gy"), None)),
        check_vma=False,
    )
```

```python
import functools

import jax
import jax.numpy as jnp
from jax import lax
from jax.experimental import pallas as pl
from jax.experimental.pallas import tpu as pltpu
from jax.sharding import PartitionSpec as P

BLOCK = 64
SOURCES = 16
ELEMENTS = 16
ROWS = 48
SLOTS = 8
ORDER = 384
EARLY = 10

LOW = 0
UPP = 64
ROW_LOW = 128
ROW_UPP = 192
SEND_UP = 256
SEND_DOWN = 272
SEND_ROW = 288
SPARE = 304
ODD = 305
TABLE = 312

VMEM = pl.BlockSpec(memory_space=pltpu.VMEM)
SMEM = pl.BlockSpec(memory_space=pltpu.SMEM)
HBM = pl.BlockSpec(memory_space=pltpu.HBM)


def params(mebibytes=24):
    return pltpu.CompilerParams(vmem_limit_bytes=mebibytes << 20)


def vmem(shape, dtype=jnp.float32):
    return pltpu.VMEM(shape, dtype)


def in_low_half(shape):
    return lax.broadcasted_iota(jnp.int32, shape, len(shape) - 1) < BLOCK


def matrix_copies(matrix, target, begin, end, sems):
    return [
        pltpu.make_async_copy(matrix.at[i], target.at[i - begin], sems.at[i - begin])
        for i in range(begin, end)
    ]


def table_kernel(ids, faces, source, matrix, table, pairs, down_x, down_y, early, owner, user, sems):
    copies = matrix_copies(matrix, early, 0, EARLY, sems)
    for copy in copies:
        copy.start()
    own = ids[0]
    for axis in range(2):
        table[ODD + axis] = ids[3 + axis]
    for row in range(3 * ROWS):
        user[row] = -1
    for element in range(ELEMENTS):
        for axis in range(3):
            at = element * 4 + axis
            row = faces[2 * axis, element] - own
            owner[row] = at
            table[ROW_LOW + at] = row
            face = faces[2 * axis + 1, element]
            row = face - own
            if axis < 2:
                here = jnp.logical_and(row >= 0, row < ROWS)
                row = jnp.where(here, row, face - ids[1 + axis])
            user[row] = element
            table[ROW_UPP + at] = row
    for group in range(ROWS // 8):
        for pair in range(8):
            pairs[pl.ds(group * 64 + pair, 8, stride=8), :] = source[
                group * 8 : group * 8 + 8, pair * 128 : pair * 128 + 128
            ]
    count = [jnp.int32(0), jnp.int32(0)]
    for row in range(ROWS):
        ref = owner[row]
        axis = ref & 3
        element = ref >> 2
        other = user[row]
        here = other >= 0
        slot = jnp.where(axis == 0, count[0], count[1])
        table[LOW + ref] = jnp.where(here, other, ELEMENTS + slot)
        table[jnp.where(here, UPP + other * 4 + axis, SPARE)] = element
        table[jnp.where(here, SPARE, SEND_DOWN + axis * SLOTS + slot)] = element
        table[jnp.where(here, SPARE, SEND_ROW + axis * SLOTS + slot)] = row
        step = jnp.where(here, 0, 1)
        count[0] = count[0] + jnp.where(axis == 0, step, 0)
        count[1] = count[1] + jnp.where(axis == 1, step, 0)
    for axis in range(2):
        slot = jnp.int32(0)
        for row in range(ROWS):
            element = user[ROWS * (1 + axis) + row]
            here = element >= 0
            at = element * 4 + axis
            table[jnp.where(here, UPP + at, SPARE)] = ELEMENTS + slot
            table[jnp.where(here, ROW_UPP + at, SPARE)] = ROWS + axis * SLOTS + slot
            table[jnp.where(here, SEND_UP + axis * SLOTS + slot, SPARE)] = element
            slot = slot + jnp.where(here, 1, 0)
    for axis, out in enumerate((down_x, down_y)):
        for slot in range(SLOTS):
            row = table[SEND_ROW + axis * SLOTS + slot]
            out[slot] = pairs[pl.ds(pl.multiple_of(row * 8, 8), 8), :]
    for copy in copies:
        copy.wait()


def split_kernel(early, matrix, high, low, late, sems):
    copies = matrix_copies(matrix, late, EARLY, ELEMENTS, sems)
    for copy in copies:
        copy.start()

    def split(full, element):
        top = full.astype(jnp.bfloat16)
        high[element] = top
        low[element] = (full - top.astype(jnp.float32)).astype(jnp.bfloat16)

    @pl.loop(0, EARLY)
    def _(element):
        split(early[element], element)

    for i, copy in enumerate(copies):
        copy.wait()
        split(late[i], EARLY + i)


def multiply(step, table, get, high, low, vector, flux, sends, moments, sums, left):
    low_half = in_low_half((SOURCES, 128))
    norm = jnp.zeros((SOURCES, 128), jnp.float32)
    energy = jnp.zeros((SOURCES, 128), jnp.float32)
    for element in range(ELEMENTS):
        tiles = []
        for axis in range(3):
            tile = get(element, axis)
            tiles.append(tile)
            if vector is not None:
                vector[element, axis] = tile
            if step < 2:
                norm = norm + tile * tile
            first = tile.astype(jnp.bfloat16)
            rest = tile - first.astype(jnp.float32)
            second = rest.astype(jnp.bfloat16)
            third = (rest - second.astype(jnp.float32)).astype(jnp.bfloat16)
            for part, value in enumerate((first, second, third)):
                left[element, part * 16 : part * 16 + 16, axis * 128 : axis * 128 + 128] = value
        rows = left[element]
        by_high = jnp.dot(rows, high[element], preferred_element_type=jnp.float32)
        by_low = jnp.dot(rows[:32], low[element], preferred_element_type=jnp.float32)
        total = by_high[0:16] + (by_high[16:32] + by_low[0:16] + (by_high[32:48] + by_low[16:32]))
        for axis in range(3):
            part = total[:, axis * 128 : axis * 128 + 128]
            flux[element, axis] = part
            if step < 2:
                energy = energy + tiles[axis] * part
    for axis in range(2):
        for slot in range(4):
            at = SEND_UP + axis * SLOTS + slot
            up = jnp.where(
                low_half, pltpu.roll(flux[table[at + 4], axis], 64, 1), flux[table[at], axis]
            )
            if step == 2:
                sends[axis][slot] = up
                continue
            at = SEND_DOWN + axis * SLOTS + slot
            down = jnp.where(
                low_half, flux[table[at], axis], pltpu.roll(flux[table[at + 4], axis], 64, 1)
            )
            odd = table[ODD + axis] == 1
            sends[2 * axis][slot] = jnp.where(odd, down, up)
            sends[2 * axis + 1][slot] = jnp.where(odd, up, down)
    if step < 2:
        sums[...] = with_moments(step, norm, energy, moments)


def with_moments(step, norm, energy, moments):
    shape = (SOURCES, 128)
    lane = lax.broadcasted_iota(jnp.int32, shape, 1)
    source = lax.broadcasted_iota(jnp.int32, shape, 0)
    half_norm = 0.5 * jnp.sum(norm, axis=1, keepdims=True)
    whole_energy = jnp.sum(energy, axis=1, keepdims=True)
    before = jnp.zeros(shape, jnp.float32) if moments is None else moments[...]
    place = lane - 2 * step * SOURCES - source
    return jnp.where(place == 0, half_norm, jnp.where(place == SOURCES, whole_energy, before))


def share_kernel(vector, flux, moments, shares):
    norm = jnp.zeros((SOURCES, 128), jnp.float32)
    energy = jnp.zeros((SOURCES, 128), jnp.float32)
    for element in range(ELEMENTS):
        for axis in range(3):
            tile = vector[element, axis]
            norm = norm + tile * tile
            energy = energy + tile * flux[element, axis]
    now = with_moments(2, norm, energy, moments)
    shares[...] = jnp.broadcast_to(jnp.sum(now, axis=0, keepdims=True), shares.shape)


def tile_of(below, above):
    low_half = in_low_half((8, 128))
    even = jnp.where(low_half, below, pltpu.roll(above, 64, 1))
    odd = jnp.where(low_half, pltpu.roll(below, 64, 1), above)
    return jnp.concatenate([even, odd], axis=0)


def first_kernel(table, pairs, ghost_x, ghost_y, high, low,
                 flux, xa, xb, ya, yb, sums, rows, left):
    for row in range(ROWS):
        rows[row] = pairs[row * 8 : row * 8 + 8, :]
    for axis, ghost in enumerate((ghost_x, ghost_y)):
        for slot in range(SLOTS):
            rows[ROWS + axis * SLOTS + slot] = ghost[slot]

    def get(element, axis):
        at = element * 4 + axis
        return tile_of(rows[table[ROW_LOW + at]], rows[table[ROW_UPP + at]])

    multiply(0, table, get, high, low, None, flux, (xa, xb, ya, yb), None, sums, left)


def gather_flux(table, previous, received, every):
    low_half = in_low_half((SOURCES, 128))
    every[0:ELEMENTS] = previous[...]
    for axis in range(2):
        ahead_low = jnp.logical_xor(low_half, table[ODD + axis] == 1)
        for slot in range(4):
            one = received[2 * axis][slot]
            two = received[2 * axis + 1][slot]
            every[ELEMENTS + slot, axis] = jnp.where(ahead_low, one, two)
            every[ELEMENTS + slot + 4, axis] = pltpu.roll(jnp.where(ahead_low, two, one), 64, 1)


def later_kernel(step, table, previous, yb, xa, xb, ya, *rest):
    if step == 1:
        moments, high, low, vector, flux, *sends, sums, every, left = rest
    else:
        high, low, vector, flux, *sends, every, left = rest
        moments = sums = None
    low_half = in_low_half((SOURCES, 128))
    gather_flux(table, previous, (xa, xb, ya, yb), every)

    def get(element, axis):
        at = element * 4 + axis
        across = jnp.where(low_half, every[table[UPP + at], axis], every[table[LOW + at], axis])
        return every[element, axis] + pltpu.roll(across, 64, 1)

    multiply(step, table, get, high, low, vector, flux, sends, moments, sums, left)


def two_sum(a, b):
    total = a + b
    part = total - a
    return total, (a - (total - part)) + (b - part)


def halves(a):
    big = 4097.0 * a
    top = big - (big - a)
    return top, a - top


def two_product(a, b):
    total = a * b
    a1, a2 = halves(a)
    b1, b2 = halves(b)
    return total, ((a1 * b1 - total) + a1 * b2 + a2 * b1) + a2 * b2


def quick(a, b):
    total = a + b
    return total, b - (total - a)


def pair_times(a, b):
    total, rest = two_product(a[0], b[0])
    return quick(total, rest + (a[0] * b[1] + a[1] * b[0]))


def pair_minus(a, b):
    total, rest = two_sum(a[0], -b[0])
    return quick(total, rest + (a[1] - b[1]))


def pair_over(a, b):
    first = a[0] / b[0]
    left = pair_minus(a, pair_times((first, jnp.zeros_like(first)), b))
    return quick(first, left[0] / b[0])


def coefficients(mu):
    centre_0 = pair_over(mu[1], mu[0])
    bent = {i: pair_minus(mu[i + 1], pair_times(centre_0, mu[i])) for i in range(1, 5)}
    slope_1 = pair_over(bent[2], bent[1])
    centre_1 = pair_minus(slope_1, centre_0)
    span_1 = pair_over(bent[1], mu[0])
    twice = {
        i: pair_minus(
            pair_minus(bent[i + 1], pair_times(centre_1, bent[i])), pair_times(span_1, mu[i])
        )
        for i in (2, 3)
    }
    centre_2 = twice[3][0] / twice[2][0] - slope_1[0]
    span_2 = twice[2][0] / bent[1][0]
    alpha_0 = 1.0 / centre_0[0]
    beta_0 = span_1[0] * alpha_0 * alpha_0
    alpha_1 = 1.0 / (centre_1[0] - span_1[0] * alpha_0)
    beta_1 = span_2 * alpha_1 * alpha_1
    alpha_2 = 1.0 / (centre_2 - span_2 * alpha_1)
    return alpha_0, beta_0, alpha_1, beta_1, alpha_2


def total_of(shares):
    parts = [(shares[i : i + 8], jnp.zeros((8, 128), jnp.float32)) for i in range(0, shares.shape[0], 8)]

    def add(a, b):
        total, lost = two_sum(a[0], b[0])
        return total, a[1] + b[1] + lost

    while len(parts) > 1:
        parts = [add(a, b) for a, b in zip(parts[::2], parts[1::2])]
    value = parts[0]
    for shift in (4, 2, 1):
        value = add(value, tuple(pltpu.roll(v, shift, 0) for v in value))
    return value


def final_kernel(table, shares, pairs, firsts, seconds, flux, prev_x, prev_y, answer, residual,
                 every, answer_pairs, residual_pairs):
    low_half = in_low_half((8, 128))
    total = total_of(shares)
    lane = lax.broadcasted_iota(jnp.int32, (8, 128), 1)
    row_of = lax.broadcasted_iota(jnp.int32, (8, 128), 0)

    def packed(tile):
        return jnp.where(low_half, tile[:8], pltpu.roll(tile[8:], 64, 1))

    def moment(part, i):
        even = jnp.sum(jnp.where(lane == i * SOURCES + row_of, total[part], 0.0), axis=1, keepdims=True)
        odd = jnp.sum(jnp.where(lane == i * SOURCES + 8 + row_of, total[part], 0.0), axis=1, keepdims=True)
        return jnp.where(low_half, even, odd)

    mu = [(moment(0, i), moment(1, i)) for i in range(6)]
    alpha_0, beta_0, alpha_1, beta_1, alpha_2 = coefficients(mu)
    every[0:ELEMENTS] = flux[...]
    for axis, prev in enumerate((prev_x, prev_y)):
        for slot in range(4):
            every[ELEMENTS + slot, axis] = prev[slot]
            every[ELEMENTS + slot + 4, axis] = pltpu.roll(prev[slot], 64, 1)
    for element in range(ELEMENTS):
        for axis in range(3):
            at = element * 4 + axis
            row = pl.ds(pl.multiple_of(table[ROW_LOW + at] * 8, 8), 8)
            other = every[table[LOW + at], axis]
            k0 = pairs[row, :]
            k1 = packed(firsts[element, axis])
            k2 = packed(seconds[element, axis])
            k3 = packed(every[element, axis]) + jnp.where(low_half, pltpu.roll(other[:8], 64, 1), other[8:])
            r1 = k0 - alpha_0 * k1
            ar1 = k1 - alpha_0 * k2
            aar1 = k2 - alpha_0 * k3
            d1 = r1 + beta_0 * k0
            ad1 = ar1 + beta_0 * k1
            aad1 = aar1 + beta_0 * k2
            r2 = r1 - alpha_1 * ad1
            ar2 = ar1 - alpha_1 * aad1
            d2 = r2 + beta_1 * d1
            ad2 = ar2 + beta_1 * ad1
            answer_pairs[row, :] = alpha_0 * k0 + (alpha_1 * d1 + alpha_2 * d2)
            residual_pairs[row, :] = r2 - alpha_2 * ad2
    for block, out in ((answer_pairs, answer), (residual_pairs, residual)):
        for group in range(ROWS // 8):
            for pair in range(8):
                out[group * 8 : group * 8 + 8, pair * 128 : pair * 128 + 128] = block[
                    pl.ds(group * 64 + pair, 8, stride=8), :
                ]


def passed(value, axis, target):
    count = lax.axis_size(axis)
    return lax.ppermute(value, axis, [(i, target(i)) for i in range(count)])


def ahead(value, axis):
    return passed(value, axis, lambda i: (i + 1) % lax.axis_size(axis))


def back(value, axis):
    return passed(value, axis, lambda i: (i - 1) % lax.axis_size(axis))


def swapped(value, axis, turn):
    count = lax.axis_size(axis)
    return passed(value, axis, lambda i: (i + 1 - 2 * ((i + turn) % 2)) % count)


def exchanged(sends):
    xa, xb, ya, yb = sends
    yb = swapped(yb, "gy", 1)
    return yb, swapped(xa, "gx", 0), swapped(xb, "gx", 1), swapped(ya, "gy", 0)


def local(heat_source, stiffness, element_faces):
    outer, inner = lax.axis_size("gx"), lax.axis_size("gy")
    at_x, at_y = lax.axis_index("gx"), lax.axis_index("gy")
    ids = jnp.stack(
        [
            (at_x * inner + at_y) * ROWS,
            ((at_x + 1) % outer * inner + at_y) * ROWS - ROWS,
            (at_x * inner + (at_y + 1) % inner) * ROWS - 2 * ROWS,
            at_x % 2,
            at_y % 2,
        ]
    ).astype(jnp.int32)
    pack = vmem((4, SOURCES, 128))
    face = vmem((SLOTS, 8, 128))
    state = vmem((ELEMENTS, 3, SOURCES, 128))
    matrix = vmem((ELEMENTS, ORDER, ORDER), jnp.bfloat16)
    moment = vmem((SOURCES, 128))
    left = pltpu.VMEM((ELEMENTS, 48, ORDER), jnp.bfloat16)
    every = pltpu.VMEM((ELEMENTS + SLOTS, 3, SOURCES, 128), jnp.float32)
    pairs_shape = (ROWS * 8, 128)

    table, pairs, down_x, down_y, early = pl.pallas_call(
        table_kernel,
        out_shape=(
            pltpu.SMEM((TABLE,), jnp.int32),
            vmem(pairs_shape),
            face,
            face,
            vmem((EARLY, ORDER, ORDER)),
        ),
        in_specs=[SMEM, SMEM, VMEM, HBM],
        out_specs=(SMEM, VMEM, VMEM, VMEM, VMEM),
        scratch_shapes=[
            pltpu.SMEM((ROWS,), jnp.int32),
            pltpu.SMEM((3 * ROWS,), jnp.int32),
            pltpu.SemaphoreType.DMA((EARLY,)),
        ],
        compiler_params=params(52),
        name="table",
    )(ids, element_faces.T, heat_source, stiffness)
    ghost_x, ghost_y = back(down_x, "gx"), back(down_y, "gy")
    high, low = pl.pallas_call(
        split_kernel,
        out_shape=(matrix, matrix),
        in_specs=[VMEM, HBM],
        out_specs=(VMEM, VMEM),
        scratch_shapes=[
            pltpu.VMEM((ELEMENTS - EARLY, ORDER, ORDER), jnp.float32),
            pltpu.SemaphoreType.DMA((ELEMENTS - EARLY,)),
        ],
        compiler_params=params(34),
        cost_estimate=pl.CostEstimate(flops=10_000_000, bytes_accessed=18 << 20, transcendentals=0),
        name="split",
    )(early, stiffness)
    flux, *sends, moments = pl.pallas_call(
        first_kernel,
        out_shape=(state, pack, pack, pack, pack, moment),
        in_specs=[SMEM] + [VMEM] * 5,
        out_specs=(VMEM,) * 6,
        scratch_shapes=[pltpu.VMEM((64, 8, 128), jnp.float32), left],
        compiler_params=params(),
        name="first",
    )(table, pairs, ghost_x, ghost_y, high, low)
    k1, flux, *sends, moments = pl.pallas_call(
        functools.partial(later_kernel, 1),
        out_shape=(state, state, pack, pack, pack, pack, moment),
        in_specs=[SMEM] + [VMEM] * 8,
        out_specs=(VMEM,) * 7,
        scratch_shapes=[every, left],
        compiler_params=params(),
        name="second",
    )(table, flux, *exchanged(sends), moments, high, low)
    k2, flux, up_x, up_y = pl.pallas_call(
        functools.partial(later_kernel, 2),
        out_shape=(state, state, pack, pack),
        in_specs=[SMEM] + [VMEM] * 7,
        out_specs=(VMEM,) * 4,
        scratch_shapes=[every, left],
        compiler_params=params(),
        name="third",
    )(table, flux, *exchanged(sends), high, low)
    shares = pl.pallas_call(
        share_kernel,
        out_shape=vmem((outer * inner, 128)),
        in_specs=[VMEM] * 3,
        out_specs=VMEM,
        compiler_params=params(),
        cost_estimate=pl.CostEstimate(flops=0, bytes_accessed=18 << 20, transcendentals=0),
        name="share",
    )(k2, flux, moments)
    prev_x, prev_y = ahead(up_x, "gx"), ahead(up_y, "gy")
    shares = lax.all_to_all(shares, ("gx", "gy"), 0, 0, tiled=True)
    natural = jax.ShapeDtypeStruct((ROWS, SOURCES * BLOCK), jnp.float32)
    return pl.pallas_call(
        final_kernel,
        out_shape=(natural, natural),
        in_specs=[SMEM] + [VMEM] * 7,
        out_specs=(VMEM, VMEM),
        scratch_shapes=[every, pltpu.VMEM(pairs_shape, jnp.float32), pltpu.VMEM(pairs_shape, jnp.float32)],
        compiler_params=params(),
        name="final",
    )(table, shares, pairs, k1, k2, flux, prev_x, prev_y)


def solution(mesh):
    return jax.shard_map(
        local,
        mesh=mesh,
        in_specs=(P(("gx", "gy"), None), P(("gx", "gy"), None, None), P(("gx", "gy"), None)),
        out_specs=(P(("gx", "gy"), None), P(("gx", "gy"), None)),
        check_vma=False,
    )
```

```python
import functools

import jax
import jax.numpy as jnp
from jax import lax
from jax.experimental import pallas as pl
from jax.experimental.pallas import tpu as pltpu
from jax.sharding import PartitionSpec as P

BLOCK = 64
SOURCES = 16
ELEMENTS = 16
ROWS = 48
SLOTS = 8
ORDER = 384
EARLY = 5

LOW = 0
UPP = 68
ROW_LOW = 132
ROW_UPP = 196
SEND_UP = 260
SEND_DOWN = 278
LIST = 9
ODD = 296
TABLE = 304

VMEM = pl.BlockSpec(memory_space=pltpu.VMEM)
SMEM = pl.BlockSpec(memory_space=pltpu.SMEM)
HBM = pl.BlockSpec(memory_space=pltpu.HBM)


def params(mebibytes=24):
    return pltpu.CompilerParams(vmem_limit_bytes=mebibytes << 20)


def vmem(shape, dtype=jnp.float32):
    return pltpu.VMEM(shape, dtype)


def in_low_half(shape):
    return lax.broadcasted_iota(jnp.int32, shape, len(shape) - 1) < BLOCK


def matrix_copies(matrix, target, begin, end, sems):
    return [
        pltpu.make_async_copy(matrix.at[i], target.at[i - begin], sems.at[i - begin])
        for i in range(begin, end)
    ]


def table_kernel(outer, inner, faces, source, matrix, table, pairs, down_x, down_y, early, owner, user, sems):
    copies = matrix_copies(matrix, early, 0, EARLY, sems)
    for copy in copies:
        copy.start()
    at_x, at_y = lax.axis_index("gx"), lax.axis_index("gy")
    own = (at_x * inner + at_y) * ROWS
    shifts = (
        (lax.rem(at_x + 1, outer) * inner + at_y) * ROWS - ROWS,
        (at_x * inner + lax.rem(at_y + 1, inner)) * ROWS - 2 * ROWS,
    )
    table[ODD] = lax.rem(at_x, 2)
    table[ODD + 1] = lax.rem(at_y, 2)
    for row in range(3 * ROWS):
        user[row] = -1
    for element in range(ELEMENTS):
        for axis in range(3):
            at = element * 4 + axis
            row = faces[2 * axis, element] - own
            owner[row] = at
            table[ROW_LOW + at] = row
            face = faces[2 * axis + 1, element]
            row = face - own
            if axis < 2:
                here = jnp.logical_and(row >= 0, row < ROWS)
                row = jnp.where(here, row, face - shifts[axis])
            user[row] = element
            table[ROW_UPP + at] = row
    for group in range(ROWS // 8):
        for pair in range(8):
            pairs[pl.ds(group * 64 + pair, 8, stride=8), :] = source[
                group * 8 : group * 8 + 8, pair * 128 : pair * 128 + 128
            ]
    ends = [jnp.int32(SEND_DOWN), jnp.int32(SEND_DOWN + LIST)]
    for row in range(ROWS):
        ref = owner[row]
        axis = ref & 3
        other = user[row]
        table[LOW + ref] = other
        table[UPP + other * 4 + axis] = ref >> 2
        table[jnp.where(axis == 0, ends[0], ends[1])] = ref
        step = jnp.where(other < 0, 1, 0)
        in_x = jnp.where(axis == 0, step, 0)
        ends = [ends[0] + in_x, ends[1] + (step - in_x)]
    for axis in range(2):
        for slot in range(SLOTS):
            table[LOW + table[SEND_DOWN + axis * LIST + slot]] = ELEMENTS + slot
        end = jnp.int32(SEND_UP + axis * LIST)
        for row in range(ROWS):
            element = user[ROWS * (1 + axis) + row]
            table[end] = element
            end = end + jnp.where(element < 0, 0, 1)
        for slot in range(SLOTS):
            at = table[SEND_UP + axis * LIST + slot] * 4 + axis
            table[UPP + at] = ELEMENTS + slot
            table[ROW_UPP + at] = ROWS + axis * SLOTS + slot
    for axis, out in enumerate((down_x, down_y)):
        for slot in range(SLOTS):
            row = table[ROW_LOW + table[SEND_DOWN + axis * LIST + slot]]
            out[slot] = pairs[pl.ds(pl.multiple_of(row * 8, 8), 8), :]
    for copy in copies:
        copy.wait()


def split_kernel(early, matrix, high, low, late, sems):
    copies = matrix_copies(matrix, late, EARLY, ELEMENTS, sems)
    for copy in copies:
        copy.start()

    def split(full, element):
        top = full.astype(jnp.bfloat16)
        high[element] = top
        low[element] = (full - top.astype(jnp.float32)).astype(jnp.bfloat16)

    @pl.loop(0, EARLY)
    def _(element):
        split(early[element], element)

    for i, copy in enumerate(copies):
        copy.wait()
        split(late[i], EARLY + i)


def multiply(step, table, get, high, low, vector, flux, sends, moments, sums, left):
    low_half = in_low_half((SOURCES, 128))
    norm = jnp.zeros((SOURCES, 128), jnp.float32)
    energy = jnp.zeros((SOURCES, 128), jnp.float32)
    for element in range(ELEMENTS):
        tiles = []
        for axis in range(3):
            tile = get(element, axis)
            tiles.append(tile)
            if vector is not None:
                vector[element, axis] = tile
            norm = norm + tile * tile
            first = tile.astype(jnp.bfloat16)
            rest = tile - first.astype(jnp.float32)
            second = rest.astype(jnp.bfloat16)
            third = (rest - second.astype(jnp.float32)).astype(jnp.bfloat16)
            for part, value in enumerate((first, second, third)):
                left[element, part * 16 : part * 16 + 16, axis * 128 : axis * 128 + 128] = value
        rows = left[element]
        by_high = jnp.dot(rows, high[element], preferred_element_type=jnp.float32)
        by_low = jnp.dot(rows[:32], low[element], preferred_element_type=jnp.float32)
        total = by_high[0:16] + (by_high[16:32] + by_low[0:16] + (by_high[32:48] + by_low[16:32]))
        for axis in range(3):
            part = total[:, axis * 128 : axis * 128 + 128]
            flux[element, axis] = part
            energy = energy + tiles[axis] * part
    for axis in range(2):
        for slot in range(4):
            at = SEND_UP + axis * LIST + slot
            up = jnp.where(
                low_half, pltpu.roll(flux[table[at + 4], axis], 64, 1), flux[table[at], axis]
            )
            if step == 2:
                sends[axis][slot] = up
                continue
            at = SEND_DOWN + axis * LIST + slot
            down = jnp.where(
                low_half, flux[table[at] >> 2, axis], pltpu.roll(flux[table[at + 4] >> 2, axis], 64, 1)
            )
            odd = table[ODD + axis] == 1
            sends[2 * axis][slot] = jnp.where(odd, down, up)
            sends[2 * axis + 1][slot] = jnp.where(odd, up, down)
    now = with_moments(step, norm, energy, moments)
    if step < 2:
        sums[...] = now
    else:
        sums[...] = jnp.broadcast_to(jnp.sum(now, axis=0, keepdims=True), sums.shape)


def with_moments(step, norm, energy, moments):
    shape = (SOURCES, 128)
    lane = lax.broadcasted_iota(jnp.int32, shape, 1)
    source = lax.broadcasted_iota(jnp.int32, shape, 0)
    half_norm = 0.5 * jnp.sum(norm, axis=1, keepdims=True)
    whole_energy = jnp.sum(energy, axis=1, keepdims=True)
    before = jnp.zeros(shape, jnp.float32) if moments is None else moments[...]
    place = lane - 2 * step * SOURCES - source
    return jnp.where(place == 0, half_norm, jnp.where(place == SOURCES, whole_energy, before))


def tile_of(below, above):
    low_half = in_low_half((8, 128))
    even = jnp.where(low_half, below, pltpu.roll(above, 64, 1))
    odd = jnp.where(low_half, pltpu.roll(below, 64, 1), above)
    return jnp.concatenate([even, odd], axis=0)


def first_kernel(table, pairs, ghost_y, ghost_x, high, low,
                 flux, xa, xb, ya, yb, sums, rows, left):
    for row in range(ROWS):
        rows[row] = pairs[row * 8 : row * 8 + 8, :]
    for axis, ghost in enumerate((ghost_x, ghost_y)):
        for slot in range(SLOTS):
            rows[ROWS + axis * SLOTS + slot] = ghost[slot]

    def get(element, axis):
        at = element * 4 + axis
        return tile_of(rows[table[ROW_LOW + at]], rows[table[ROW_UPP + at]])

    multiply(0, table, get, high, low, None, flux, (xa, xb, ya, yb), None, sums, left)


def gather_flux(table, previous, received, every):
    low_half = in_low_half((SOURCES, 128))
    every[0:ELEMENTS] = previous[...]
    for axis in range(2):
        ahead_low = jnp.logical_xor(low_half, table[ODD + axis] == 1)
        for slot in range(4):
            one = received[2 * axis][slot]
            two = received[2 * axis + 1][slot]
            every[ELEMENTS + slot, axis] = jnp.where(ahead_low, one, two)
            every[ELEMENTS + slot + 4, axis] = pltpu.roll(jnp.where(ahead_low, two, one), 64, 1)


def later_kernel(step, table, previous, yb, xa, xb, ya, moments, high, low, vector, flux, *rest):
    *sends, sums, every, left = rest
    low_half = in_low_half((SOURCES, 128))
    gather_flux(table, previous, (xa, xb, ya, yb), every)

    def get(element, axis):
        at = element * 4 + axis
        across = jnp.where(low_half, every[table[UPP + at], axis], every[table[LOW + at], axis])
        return every[element, axis] + pltpu.roll(across, 64, 1)

    multiply(step, table, get, high, low, vector, flux, sends, moments, sums, left)


def two_sum(a, b):
    total = a + b
    part = total - a
    return total, (a - (total - part)) + (b - part)


def halves(a):
    big = 4097.0 * a
    top = big - (big - a)
    return top, a - top


def two_product(a, b):
    total = a * b
    a1, a2 = halves(a)
    b1, b2 = halves(b)
    return total, ((a1 * b1 - total) + a1 * b2 + a2 * b1) + a2 * b2


def quick(a, b):
    total = a + b
    return total, b - (total - a)


def pair_times(a, b):
    total, rest = two_product(a[0], b[0])
    return quick(total, rest + (a[0] * b[1] + a[1] * b[0]))


def pair_minus(a, b):
    total, rest = two_sum(a[0], -b[0])
    return quick(total, rest + (a[1] - b[1]))


def pair_over(a, b):
    first = a[0] / b[0]
    left = pair_minus(a, pair_times((first, jnp.zeros_like(first)), b))
    return quick(first, left[0] / b[0])


def coefficients(mu):
    centre_0 = pair_over(mu[1], mu[0])
    bent = {i: pair_minus(mu[i + 1], pair_times(centre_0, mu[i])) for i in range(1, 5)}
    slope_1 = pair_over(bent[2], bent[1])
    centre_1 = pair_minus(slope_1, centre_0)
    span_1 = pair_over(bent[1], mu[0])
    twice = {
        i: pair_minus(
            pair_minus(bent[i + 1], pair_times(centre_1, bent[i])), pair_times(span_1, mu[i])
        )
        for i in (2, 3)
    }
    centre_2 = twice[3][0] / twice[2][0] - slope_1[0]
    span_2 = twice[2][0] / bent[1][0]
    alpha_0 = 1.0 / centre_0[0]
    beta_0 = span_1[0] * alpha_0 * alpha_0
    alpha_1 = 1.0 / (centre_1[0] - span_1[0] * alpha_0)
    beta_1 = span_2 * alpha_1 * alpha_1
    alpha_2 = 1.0 / (centre_2 - span_2 * alpha_1)
    return alpha_0, beta_0, alpha_1, beta_1, alpha_2


def total_of(shares):
    parts = [(shares[i : i + 8], jnp.zeros((8, 128), jnp.float32)) for i in range(0, shares.shape[0], 8)]

    def add(a, b):
        total, lost = two_sum(a[0], b[0])
        return total, a[1] + b[1] + lost

    while len(parts) > 1:
        parts = [add(a, b) for a, b in zip(parts[::2], parts[1::2])]
    value = parts[0]
    for shift in (4, 2, 1):
        value = add(value, tuple(pltpu.roll(v, shift, 0) for v in value))
    return value


def final_kernel(table, shares, pairs, firsts, seconds, flux, prev_x, prev_y, answer, residual,
                 every, answer_pairs, residual_pairs):
    low_half = in_low_half((8, 128))
    total = total_of(shares)
    lane = lax.broadcasted_iota(jnp.int32, (8, 128), 1)
    row_of = lax.broadcasted_iota(jnp.int32, (8, 128), 0)

    def packed(tile):
        return jnp.where(low_half, tile[:8], pltpu.roll(tile[8:], 64, 1))

    def moment(part, i):
        even = jnp.sum(jnp.where(lane == i * SOURCES + row_of, total[part], 0.0), axis=1, keepdims=True)
        odd = jnp.sum(jnp.where(lane == i * SOURCES + 8 + row_of, total[part], 0.0), axis=1, keepdims=True)
        return jnp.where(low_half, even, odd)

    mu = [(moment(0, i), moment(1, i)) for i in range(6)]
    alpha_0, beta_0, alpha_1, beta_1, alpha_2 = coefficients(mu)
    every[0:ELEMENTS] = flux[...]
    for axis, prev in enumerate((prev_x, prev_y)):
        for slot in range(4):
            every[ELEMENTS + slot, axis] = prev[slot]
            every[ELEMENTS + slot + 4, axis] = pltpu.roll(prev[slot], 64, 1)
    for element in range(ELEMENTS):
        for axis in range(3):
            at = element * 4 + axis
            row = pl.ds(pl.multiple_of(table[ROW_LOW + at] * 8, 8), 8)
            other = every[table[LOW + at], axis]
            k0 = pairs[row, :]
            k1 = packed(firsts[element, axis])
            k2 = packed(seconds[element, axis])
            k3 = packed(every[element, axis]) + jnp.where(low_half, pltpu.roll(other[:8], 64, 1), other[8:])
            r1 = k0 - alpha_0 * k1
            ar1 = k1 - alpha_0 * k2
            aar1 = k2 - alpha_0 * k3
            d1 = r1 + beta_0 * k0
            ad1 = ar1 + beta_0 * k1
            aad1 = aar1 + beta_0 * k2
            r2 = r1 - alpha_1 * ad1
            ar2 = ar1 - alpha_1 * aad1
            d2 = r2 + beta_1 * d1
            ad2 = ar2 + beta_1 * ad1
            answer_pairs[row, :] = alpha_0 * k0 + (alpha_1 * d1 + alpha_2 * d2)
            residual_pairs[row, :] = r2 - alpha_2 * ad2
    for block, out in ((answer_pairs, answer), (residual_pairs, residual)):
        for group in range(ROWS // 8):
            for pair in range(8):
                out[group * 8 : group * 8 + 8, pair * 128 : pair * 128 + 128] = block[
                    pl.ds(group * 64 + pair, 8, stride=8), :
                ]


def passed(value, axis, target):
    count = lax.axis_size(axis)
    return lax.ppermute(value, axis, [(i, target(i)) for i in range(count)])


def ahead(value, axis):
    return passed(value, axis, lambda i: (i + 1) % lax.axis_size(axis))


def back(value, axis):
    return passed(value, axis, lambda i: (i - 1) % lax.axis_size(axis))


def swapped(value, axis, turn):
    count = lax.axis_size(axis)
    return passed(value, axis, lambda i: (i + 1 - 2 * ((i + turn) % 2)) % count)


def exchanged(sends):
    xa, xb, ya, yb = sends
    yb = swapped(yb, "gy", 1)
    return yb, swapped(xa, "gx", 0), swapped(xb, "gx", 1), swapped(ya, "gy", 0)


def local(heat_source, stiffness, element_faces):
    outer, inner = lax.axis_size("gx"), lax.axis_size("gy")
    pack = vmem((4, SOURCES, 128))
    face = vmem((SLOTS, 8, 128))
    state = vmem((ELEMENTS, 3, SOURCES, 128))
    matrix = vmem((ELEMENTS, ORDER, ORDER), jnp.bfloat16)
    moment = vmem((SOURCES, 128))
    left = pltpu.VMEM((ELEMENTS, 48, ORDER), jnp.bfloat16)
    every = pltpu.VMEM((ELEMENTS + SLOTS, 3, SOURCES, 128), jnp.float32)
    pairs_shape = (ROWS * 8, 128)

    table, pairs, down_x, down_y, early = pl.pallas_call(
        functools.partial(table_kernel, outer, inner),
        out_shape=(
            pltpu.SMEM((TABLE,), jnp.int32),
            vmem(pairs_shape),
            face,
            face,
            vmem((EARLY, ORDER, ORDER)),
        ),
        in_specs=[SMEM, VMEM, HBM],
        out_specs=(SMEM, VMEM, VMEM, VMEM, VMEM),
        scratch_shapes=[
            pltpu.SMEM((ROWS,), jnp.int32),
            pltpu.SMEM((3 * ROWS,), jnp.int32),
            pltpu.SemaphoreType.DMA((EARLY,)),
        ],
        compiler_params=params(52),
        name="table",
    )(element_faces.T, heat_source, stiffness)
    ghost_y = back(down_y, "gy")
    ghost_x = back(down_x, "gx")
    high, low = pl.pallas_call(
        split_kernel,
        out_shape=(matrix, matrix),
        in_specs=[VMEM, HBM],
        out_specs=(VMEM, VMEM),
        scratch_shapes=[
            pltpu.VMEM((ELEMENTS - EARLY, ORDER, ORDER), jnp.float32),
            pltpu.SemaphoreType.DMA((ELEMENTS - EARLY,)),
        ],
        compiler_params=params(34),
        cost_estimate=pl.CostEstimate(flops=10_000_000, bytes_accessed=18 << 20, transcendentals=0),
        name="split",
    )(early, stiffness)
    flux, *sends, moments = pl.pallas_call(
        first_kernel,
        out_shape=(state, pack, pack, pack, pack, moment),
        in_specs=[SMEM] + [VMEM] * 5,
        out_specs=(VMEM,) * 6,
        scratch_shapes=[pltpu.VMEM((64, 8, 128), jnp.float32), left],
        compiler_params=params(),
        name="first",
    )(table, pairs, ghost_y, ghost_x, high, low)
    k1, flux, *sends, moments = pl.pallas_call(
        functools.partial(later_kernel, 1),
        out_shape=(state, state, pack, pack, pack, pack, moment),
        in_specs=[SMEM] + [VMEM] * 8,
        out_specs=(VMEM,) * 7,
        scratch_shapes=[every, left],
        compiler_params=params(),
        name="second",
    )(table, flux, *exchanged(sends), moments, high, low)
    k2, flux, up_x, up_y, shares = pl.pallas_call(
        functools.partial(later_kernel, 2),
        out_shape=(state, state, pack, pack, vmem((outer * inner, 128))),
        in_specs=[SMEM] + [VMEM] * 8,
        out_specs=(VMEM,) * 5,
        scratch_shapes=[every, left],
        compiler_params=params(),
        name="third",
    )(table, flux, *exchanged(sends), moments, high, low)
    prev_x, prev_y = ahead(up_x, "gx"), ahead(up_y, "gy")
    shares = lax.all_to_all(shares, ("gx", "gy"), 0, 0, tiled=True)
    natural = jax.ShapeDtypeStruct((ROWS, SOURCES * BLOCK), jnp.float32)
    return pl.pallas_call(
        final_kernel,
        out_shape=(natural, natural),
        in_specs=[SMEM] + [VMEM] * 7,
        out_specs=(VMEM, VMEM),
        scratch_shapes=[every, pltpu.VMEM(pairs_shape, jnp.float32), pltpu.VMEM(pairs_shape, jnp.float32)],
        compiler_params=params(),
        name="final",
    )(table, shares, pairs, k1, k2, flux, prev_x, prev_y)


def solution(mesh):
    return jax.shard_map(
        local,
        mesh=mesh,
        in_specs=(P(("gx", "gy"), None), P(("gx", "gy"), None, None), P(("gx", "gy"), None)),
        out_specs=(P(("gx", "gy"), None), P(("gx", "gy"), None)),
        check_vma=False,
    )
```

```python
import functools

import jax
import jax.numpy as jnp
from jax import lax
from jax.experimental import pallas as pl
from jax.experimental.pallas import tpu as pltpu
from jax.sharding import PartitionSpec as P

BLOCK = 64
SOURCES = 16
ELEMENTS = 16
ROWS = 48
SLOTS = 8
ORDER = 384
EARLY = 5

LOW = 0
UPP = 68
ROW_LOW = 132
ROW_UPP = 196
SEND_UP = 260
SEND_DOWN = 278
LIST = 9
ODD = 296
TABLE = 304

VMEM = pl.BlockSpec(memory_space=pltpu.VMEM)
SMEM = pl.BlockSpec(memory_space=pltpu.SMEM)
HBM = pl.BlockSpec(memory_space=pltpu.HBM)


def params(mebibytes=24):
    return pltpu.CompilerParams(vmem_limit_bytes=mebibytes << 20)


def vmem(shape, dtype=jnp.float32):
    return pltpu.VMEM(shape, dtype)


def in_low_half(shape):
    return lax.broadcasted_iota(jnp.int32, shape, len(shape) - 1) < BLOCK


def matrix_copies(matrix, target, begin, end, sems):
    return [
        pltpu.make_async_copy(matrix.at[i], target.at[i - begin], sems.at[i - begin])
        for i in range(begin, end)
    ]


def table_kernel(outer, inner, faces_hbm, source_hbm, matrix, table, pairs, down_x, down_y, early,
                 owner, user, faces, source, sems, faces_sem, source_sem):
    faces_copy = pltpu.make_async_copy(faces_hbm, faces, faces_sem)
    source_copy = pltpu.make_async_copy(source_hbm, source, source_sem)
    faces_copy.start()
    source_copy.start()
    copies = matrix_copies(matrix, early, 0, EARLY, sems)
    for copy in copies:
        copy.start()
    at_x, at_y = lax.axis_index("gx"), lax.axis_index("gy")
    own = (at_x * inner + at_y) * ROWS
    shifts = (
        (lax.rem(at_x + 1, outer) * inner + at_y) * ROWS - ROWS,
        (at_x * inner + lax.rem(at_y + 1, inner)) * ROWS - 2 * ROWS,
    )
    table[ODD] = lax.rem(at_x, 2)
    table[ODD + 1] = lax.rem(at_y, 2)
    for row in range(3 * ROWS):
        user[row] = -1
    faces_copy.wait()
    for element in range(ELEMENTS):
        for axis in range(3):
            at = element * 4 + axis
            row = faces[2 * axis, element] - own
            owner[row] = at
            table[ROW_LOW + at] = row
            face = faces[2 * axis + 1, element]
            row = face - own
            if axis < 2:
                here = jnp.logical_and(row >= 0, row < ROWS)
                row = jnp.where(here, row, face - shifts[axis])
            user[row] = element
            table[ROW_UPP + at] = row
    ends = [jnp.int32(SEND_DOWN), jnp.int32(SEND_DOWN + LIST)]
    for row in range(ROWS):
        ref = owner[row]
        axis = ref & 3
        other = user[row]
        table[LOW + ref] = other
        table[UPP + other * 4 + axis] = ref >> 2
        table[jnp.where(axis == 0, ends[0], ends[1])] = ref
        step = jnp.where(other < 0, 1, 0)
        in_x = jnp.where(axis == 0, step, 0)
        ends = [ends[0] + in_x, ends[1] + (step - in_x)]
    for axis in range(2):
        for slot in range(SLOTS):
            table[LOW + table[SEND_DOWN + axis * LIST + slot]] = ELEMENTS + slot
        end = jnp.int32(SEND_UP + axis * LIST)
        for row in range(ROWS):
            element = user[ROWS * (1 + axis) + row]
            table[end] = element
            end = end + jnp.where(element < 0, 0, 1)
        for slot in range(SLOTS):
            at = table[SEND_UP + axis * LIST + slot] * 4 + axis
            table[UPP + at] = ELEMENTS + slot
            table[ROW_UPP + at] = ROWS + axis * SLOTS + slot
    source_copy.wait()
    for group in range(ROWS // 8):
        for pair in range(8):
            pairs[pl.ds(group * 64 + pair, 8, stride=8), :] = source[
                group * 8 : group * 8 + 8, pair * 128 : pair * 128 + 128
            ]
    for axis, out in enumerate((down_x, down_y)):
        for slot in range(SLOTS):
            row = table[ROW_LOW + table[SEND_DOWN + axis * LIST + slot]]
            out[slot] = pairs[pl.ds(pl.multiple_of(row * 8, 8), 8), :]
    for copy in copies:
        copy.wait()


def split_kernel(early, matrix, parts, late, sems):
    copies = matrix_copies(matrix, late, EARLY, ELEMENTS, sems)
    for copy in copies:
        copy.start()

    def split(full, element):
        top = full.astype(jnp.bfloat16)
        parts[element, :ORDER] = top
        parts[element, ORDER:] = (full - top.astype(jnp.float32)).astype(jnp.bfloat16)

    @pl.loop(0, EARLY)
    def _(element):
        split(early[element], element)

    for i, copy in enumerate(copies):
        copy.wait()
        split(late[i], EARLY + i)


def multiply(step, table, get, parts, vector, flux, sends, moments, sums, left):
    low_half = in_low_half((SOURCES, 128))
    norm = jnp.zeros((SOURCES, 128), jnp.float32)
    energy = jnp.zeros((SOURCES, 128), jnp.float32)
    for element in range(ELEMENTS):
        tiles = []
        for axis in range(3):
            tile = get(element, axis)
            tiles.append(tile)
            if vector is not None:
                vector[element, axis] = tile
            norm = norm + tile * tile
            first = tile.astype(jnp.bfloat16)
            rest = tile - first.astype(jnp.float32)
            second = rest.astype(jnp.bfloat16)
            third = (rest - second.astype(jnp.float32)).astype(jnp.bfloat16)
            for part, value in enumerate((first, second, third)):
                for begin in (axis * 128, ORDER + axis * 128):
                    left[element, part * 16 : part * 16 + 16, begin : begin + 128] = value
        for axis in range(3):
            product = jnp.dot(
                left[element],
                parts[element, :, axis * 128 : axis * 128 + 128],
                preferred_element_type=jnp.float32,
            )
            part = product[0:16] + (product[16:32] + product[32:48])
            flux[element, axis] = part
            energy = energy + tiles[axis] * part
    for axis in range(2):
        for slot in range(4):
            at = SEND_UP + axis * LIST + slot
            up = jnp.where(
                low_half, pltpu.roll(flux[table[at + 4], axis], 64, 1), flux[table[at], axis]
            )
            if step == 2:
                sends[axis][slot] = up
                continue
            at = SEND_DOWN + axis * LIST + slot
            down = jnp.where(
                low_half, flux[table[at] >> 2, axis], pltpu.roll(flux[table[at + 4] >> 2, axis], 64, 1)
            )
            odd = table[ODD + axis] == 1
            sends[2 * axis][slot] = jnp.where(odd, down, up)
            sends[2 * axis + 1][slot] = jnp.where(odd, up, down)
    now = with_moments(step, norm, energy, moments)
    if step < 2:
        sums[...] = now
    else:
        sums[...] = jnp.broadcast_to(jnp.sum(now, axis=0, keepdims=True), sums.shape)


def with_moments(step, norm, energy, moments):
    shape = (SOURCES, 128)
    lane = lax.broadcasted_iota(jnp.int32, shape, 1)
    source = lax.broadcasted_iota(jnp.int32, shape, 0)
    half_norm = 0.5 * jnp.sum(norm, axis=1, keepdims=True)
    whole_energy = jnp.sum(energy, axis=1, keepdims=True)
    before = jnp.zeros(shape, jnp.float32) if moments is None else moments[...]
    place = lane - 2 * step * SOURCES - source
    return jnp.where(place == 0, half_norm, jnp.where(place == SOURCES, whole_energy, before))


def tile_of(below, above):
    low_half = in_low_half((8, 128))
    even = jnp.where(low_half, below, pltpu.roll(above, 64, 1))
    odd = jnp.where(low_half, pltpu.roll(below, 64, 1), above)
    return jnp.concatenate([even, odd], axis=0)


def first_kernel(table, pairs, ghost_y, ghost_x, parts,
                 flux, xa, xb, ya, yb, sums, rows, left):
    for row in range(ROWS):
        rows[row] = pairs[row * 8 : row * 8 + 8, :]
    for axis, ghost in enumerate((ghost_x, ghost_y)):
        for slot in range(SLOTS):
            rows[ROWS + axis * SLOTS + slot] = ghost[slot]

    def get(element, axis):
        at = element * 4 + axis
        return tile_of(rows[table[ROW_LOW + at]], rows[table[ROW_UPP + at]])

    multiply(0, table, get, parts, None, flux, (xa, xb, ya, yb), None, sums, left)


def gather_flux(table, previous, received, every):
    low_half = in_low_half((SOURCES, 128))
    every[0:ELEMENTS] = previous[...]
    for axis in range(2):
        ahead_low = jnp.logical_xor(low_half, table[ODD + axis] == 1)
        for slot in range(4):
            one = received[2 * axis][slot]
            two = received[2 * axis + 1][slot]
            every[ELEMENTS + slot, axis] = jnp.where(ahead_low, one, two)
            every[ELEMENTS + slot + 4, axis] = pltpu.roll(jnp.where(ahead_low, two, one), 64, 1)


def later_kernel(step, table, previous, yb, xa, xb, ya, moments, parts, vector, flux, *rest):
    *sends, sums, every, left = rest
    low_half = in_low_half((SOURCES, 128))
    gather_flux(table, previous, (xa, xb, ya, yb), every)

    def get(element, axis):
        at = element * 4 + axis
        across = jnp.where(low_half, every[table[UPP + at], axis], every[table[LOW + at], axis])
        return every[element, axis] + pltpu.roll(across, 64, 1)

    multiply(step, table, get, parts, vector, flux, sends, moments, sums, left)


def two_sum(a, b):
    total = a + b
    part = total - a
    return total, (a - (total - part)) + (b - part)


def halves(a):
    big = 4097.0 * a
    top = big - (big - a)
    return top, a - top


def two_product(a, b):
    total = a * b
    a1, a2 = halves(a)
    b1, b2 = halves(b)
    return total, ((a1 * b1 - total) + a1 * b2 + a2 * b1) + a2 * b2


def quick(a, b):
    total = a + b
    return total, b - (total - a)


def pair_times(a, b):
    total, rest = two_product(a[0], b[0])
    return quick(total, rest + (a[0] * b[1] + a[1] * b[0]))


def pair_minus(a, b):
    total, rest = two_sum(a[0], -b[0])
    return quick(total, rest + (a[1] - b[1]))


def pair_over(a, b):
    first = a[0] / b[0]
    left = pair_minus(a, pair_times((first, jnp.zeros_like(first)), b))
    return quick(first, left[0] / b[0])


def coefficients(mu):
    centre_0 = pair_over(mu[1], mu[0])
    bent = {i: pair_minus(mu[i + 1], pair_times(centre_0, mu[i])) for i in range(1, 5)}
    slope_1 = pair_over(bent[2], bent[1])
    centre_1 = pair_minus(slope_1, centre_0)
    span_1 = pair_over(bent[1], mu[0])
    twice = {
        i: pair_minus(
            pair_minus(bent[i + 1], pair_times(centre_1, bent[i])), pair_times(span_1, mu[i])
        )
        for i in (2, 3)
    }
    centre_2 = twice[3][0] / twice[2][0] - slope_1[0]
    span_2 = twice[2][0] / bent[1][0]
    alpha_0 = 1.0 / centre_0[0]
    beta_0 = span_1[0] * alpha_0 * alpha_0
    alpha_1 = 1.0 / (centre_1[0] - span_1[0] * alpha_0)
    beta_1 = span_2 * alpha_1 * alpha_1
    alpha_2 = 1.0 / (centre_2 - span_2 * alpha_1)
    return alpha_0, beta_0, alpha_1, beta_1, alpha_2


def total_of(shares):
    parts = [(shares[i : i + 8], jnp.zeros((8, 128), jnp.float32)) for i in range(0, shares.shape[0], 8)]

    def add(a, b):
        total, lost = two_sum(a[0], b[0])
        return total, a[1] + b[1] + lost

    while len(parts) > 1:
        parts = [add(a, b) for a, b in zip(parts[::2], parts[1::2])]
    value = parts[0]
    for shift in (4, 2, 1):
        value = add(value, tuple(pltpu.roll(v, shift, 0) for v in value))
    return value


def final_kernel(table, shares, pairs, firsts, seconds, flux, prev_x, prev_y, answer, residual,
                 every, answer_pairs, residual_pairs):
    low_half = in_low_half((8, 128))
    total = total_of(shares)
    lane = lax.broadcasted_iota(jnp.int32, (8, 128), 1)
    row_of = lax.broadcasted_iota(jnp.int32, (8, 128), 0)

    def packed(tile):
        return jnp.where(low_half, tile[:8], pltpu.roll(tile[8:], 64, 1))

    def moment(part, i):
        even = jnp.sum(jnp.where(lane == i * SOURCES + row_of, total[part], 0.0), axis=1, keepdims=True)
        odd = jnp.sum(jnp.where(lane == i * SOURCES + 8 + row_of, total[part], 0.0), axis=1, keepdims=True)
        return jnp.where(low_half, even, odd)

    mu = [(moment(0, i), moment(1, i)) for i in range(6)]
    alpha_0, beta_0, alpha_1, beta_1, alpha_2 = coefficients(mu)
    every[0:ELEMENTS] = flux[...]
    for axis, prev in enumerate((prev_x, prev_y)):
        for slot in range(4):
            every[ELEMENTS + slot, axis] = prev[slot]
            every[ELEMENTS + slot + 4, axis] = pltpu.roll(prev[slot], 64, 1)
    for element in range(ELEMENTS):
        for axis in range(3):
            at = element * 4 + axis
            row = pl.ds(pl.multiple_of(table[ROW_LOW + at] * 8, 8), 8)
            other = every[table[LOW + at], axis]
            k0 = pairs[row, :]
            k1 = packed(firsts[element, axis])
            k2 = packed(seconds[element, axis])
            k3 = packed(every[element, axis]) + jnp.where(low_half, pltpu.roll(other[:8], 64, 1), other[8:])
            r1 = k0 - alpha_0 * k1
            ar1 = k1 - alpha_0 * k2
            aar1 = k2 - alpha_0 * k3
            d1 = r1 + beta_0 * k0
            ad1 = ar1 + beta_0 * k1
            aad1 = aar1 + beta_0 * k2
            r2 = r1 - alpha_1 * ad1
            ar2 = ar1 - alpha_1 * aad1
            d2 = r2 + beta_1 * d1
            ad2 = ar2 + beta_1 * ad1
            answer_pairs[row, :] = alpha_0 * k0 + (alpha_1 * d1 + alpha_2 * d2)
            residual_pairs[row, :] = r2 - alpha_2 * ad2
    for block, out in ((answer_pairs, answer), (residual_pairs, residual)):
        for group in range(ROWS // 8):
            for pair in range(8):
                out[group * 8 : group * 8 + 8, pair * 128 : pair * 128 + 128] = block[
                    pl.ds(group * 64 + pair, 8, stride=8), :
                ]


def passed(value, axis, target):
    count = lax.axis_size(axis)
    return lax.ppermute(value, axis, [(i, target(i)) for i in range(count)])


def ahead(value, axis):
    return passed(value, axis, lambda i: (i + 1) % lax.axis_size(axis))


def back(value, axis):
    return passed(value, axis, lambda i: (i - 1) % lax.axis_size(axis))


def swapped(value, axis, turn):
    count = lax.axis_size(axis)
    return passed(value, axis, lambda i: (i + 1 - 2 * ((i + turn) % 2)) % count)


def exchanged(sends):
    xa, xb, ya, yb = sends
    yb = swapped(yb, "gy", 1)
    return yb, swapped(xa, "gx", 0), swapped(xb, "gx", 1), swapped(ya, "gy", 0)


def local(heat_source, stiffness, element_faces):
    outer, inner = lax.axis_size("gx"), lax.axis_size("gy")
    pack = vmem((4, SOURCES, 128))
    face = vmem((SLOTS, 8, 128))
    state = vmem((ELEMENTS, 3, SOURCES, 128))
    matrix = vmem((ELEMENTS, 2 * ORDER, ORDER), jnp.bfloat16)
    moment = vmem((SOURCES, 128))
    left = pltpu.VMEM((ELEMENTS, 48, 2 * ORDER), jnp.bfloat16)
    every = pltpu.VMEM((ELEMENTS + SLOTS, 3, SOURCES, 128), jnp.float32)
    pairs_shape = (ROWS * 8, 128)

    table, pairs, down_x, down_y, early = pl.pallas_call(
        functools.partial(table_kernel, outer, inner),
        out_shape=(
            pltpu.SMEM((TABLE,), jnp.int32),
            vmem(pairs_shape),
            face,
            face,
            vmem((EARLY, ORDER, ORDER)),
        ),
        in_specs=[HBM, HBM, HBM],
        out_specs=(SMEM, VMEM, VMEM, VMEM, VMEM),
        scratch_shapes=[
            pltpu.SMEM((ROWS,), jnp.int32),
            pltpu.SMEM((3 * ROWS,), jnp.int32),
            pltpu.SMEM((6, ELEMENTS), jnp.int32),
            pltpu.VMEM((ROWS, SOURCES * BLOCK), jnp.float32),
            pltpu.SemaphoreType.DMA((EARLY,)),
            pltpu.SemaphoreType.DMA,
            pltpu.SemaphoreType.DMA,
        ],
        compiler_params=params(52),
        name="table",
    )(element_faces.T, heat_source, stiffness)
    ghost_y = back(down_y, "gy")
    ghost_x = back(down_x, "gx")
    parts = pl.pallas_call(
        split_kernel,
        out_shape=matrix,
        in_specs=[VMEM, HBM],
        out_specs=VMEM,
        scratch_shapes=[
            pltpu.VMEM((ELEMENTS - EARLY, ORDER, ORDER), jnp.float32),
            pltpu.SemaphoreType.DMA((ELEMENTS - EARLY,)),
        ],
        compiler_params=params(34),
        cost_estimate=pl.CostEstimate(flops=10_000_000, bytes_accessed=18 << 20, transcendentals=0),
        name="split",
    )(early, stiffness)
    flux, *sends, moments = pl.pallas_call(
        first_kernel,
        out_shape=(state, pack, pack, pack, pack, moment),
        in_specs=[SMEM] + [VMEM] * 4,
        out_specs=(VMEM,) * 6,
        scratch_shapes=[pltpu.VMEM((64, 8, 128), jnp.float32), left],
        compiler_params=params(),
        name="first",
    )(table, pairs, ghost_y, ghost_x, parts)
    k1, flux, *sends, moments = pl.pallas_call(
        functools.partial(later_kernel, 1),
        out_shape=(state, state, pack, pack, pack, pack, moment),
        in_specs=[SMEM] + [VMEM] * 7,
        out_specs=(VMEM,) * 7,
        scratch_shapes=[every, left],
        compiler_params=params(),
        name="second",
    )(table, flux, *exchanged(sends), moments, parts)
    k2, flux, up_x, up_y, shares = pl.pallas_call(
        functools.partial(later_kernel, 2),
        out_shape=(state, state, pack, pack, vmem((outer * inner, 128))),
        in_specs=[SMEM] + [VMEM] * 7,
        out_specs=(VMEM,) * 5,
        scratch_shapes=[every, left],
        compiler_params=params(),
        name="third",
    )(table, flux, *exchanged(sends), moments, parts)
    prev_x, prev_y = ahead(up_x, "gx"), ahead(up_y, "gy")
    shares = lax.all_to_all(shares, ("gx", "gy"), 0, 0, tiled=True)
    natural = jax.ShapeDtypeStruct((ROWS, SOURCES * BLOCK), jnp.float32)
    return pl.pallas_call(
        final_kernel,
        out_shape=(natural, natural),
        in_specs=[SMEM] + [VMEM] * 7,
        out_specs=(VMEM, VMEM),
        scratch_shapes=[every, pltpu.VMEM(pairs_shape, jnp.float32), pltpu.VMEM(pairs_shape, jnp.float32)],
        compiler_params=params(),
        name="final",
    )(table, shares, pairs, k1, k2, flux, prev_x, prev_y)


def solution(mesh):
    return jax.shard_map(
        local,
        mesh=mesh,
        in_specs=(P(("gx", "gy"), None), P(("gx", "gy"), None, None), P(("gx", "gy"), None)),
        out_specs=(P(("gx", "gy"), None), P(("gx", "gy"), None)),
        check_vma=False,
    )
```

```python
import functools

import jax
import jax.numpy as jnp
from jax import lax
from jax.experimental import pallas as pl
from jax.experimental.pallas import tpu as pltpu
from jax.sharding import PartitionSpec as P

BLOCK = 64
SOURCES = 16
ELEMENTS = 16
ROWS = 48
SLOTS = 8
ORDER = 384
EARLY = 6

LOW = 0
UPP = 68
ROW_LOW = 132
ROW_UPP = 196
SEND_UP = 260
SEND_DOWN = 278
LIST = 9
ODD = 296
TABLE = 304

VMEM = pl.BlockSpec(memory_space=pltpu.VMEM)
SMEM = pl.BlockSpec(memory_space=pltpu.SMEM)
HBM = pl.BlockSpec(memory_space=pltpu.HBM)


def params(mebibytes=24):
    return pltpu.CompilerParams(vmem_limit_bytes=mebibytes << 20)


def vmem(shape, dtype=jnp.float32):
    return pltpu.VMEM(shape, dtype)


def in_low_half(shape):
    return lax.broadcasted_iota(jnp.int32, shape, len(shape) - 1) < BLOCK


def into_pairs(source, pairs, first):
    for group in range(ROWS // 8):
        for pair in range(8):
            pairs[pl.ds((first + group * 8) * 8 + pair, 8, stride=8), :] = source[
                group * 8 : group * 8 + 8, pair * 128 : pair * 128 + 128
            ]


def matrix_copies(matrix, target, begin, end, sems):
    return [
        pltpu.make_async_copy(matrix.at[i], target.at[i - begin], sems.at[i - begin])
        for i in range(begin, end)
    ]


def table_kernel(outer, inner, faces_hbm, source_hbm, matrix, table, pairs, down_x, early,
                 owner, user, faces, source, sems, faces_sem, source_sem):
    faces_copy = pltpu.make_async_copy(faces_hbm, faces, faces_sem)
    source_copy = pltpu.make_async_copy(source_hbm, source, source_sem)
    faces_copy.start()
    source_copy.start()
    copies = matrix_copies(matrix, early, 0, EARLY, sems)
    for copy in copies:
        copy.start()
    at_x, at_y = lax.axis_index("gx"), lax.axis_index("gy")
    own = (at_x * inner + at_y) * ROWS
    shifts = (
        (lax.rem(at_x + 1, outer) * inner + at_y) * ROWS - ROWS,
        (at_x * inner + lax.rem(at_y + 1, inner)) * ROWS - 2 * ROWS,
    )
    table[ODD] = lax.rem(at_x, 2)
    table[ODD + 1] = lax.rem(at_y, 2)
    for row in range(3 * ROWS):
        user[row] = -1
    faces_copy.wait()
    for element in range(ELEMENTS):
        for axis in range(3):
            at = element * 4 + axis
            row = faces[2 * axis, element] - own
            owner[row] = at
            table[ROW_LOW + at] = row
            face = faces[2 * axis + 1, element]
            row = face - own
            if axis < 2:
                here = jnp.logical_and(row >= 0, row < ROWS)
                row = jnp.where(here, row, face - shifts[axis])
            user[row] = element
            if axis == 1:
                row = jnp.where(here, row, row - (ROWS - SLOTS))
            table[ROW_UPP + at] = row
    ends = [jnp.int32(SEND_DOWN), jnp.int32(SEND_DOWN + LIST)]
    for row in range(ROWS):
        ref = owner[row]
        axis = ref & 3
        other = user[row]
        table[LOW + ref] = other
        table[UPP + other * 4 + axis] = ref >> 2
        table[jnp.where(axis == 0, ends[0], ends[1])] = ref
        step = jnp.where(other < 0, 1, 0)
        in_x = jnp.where(axis == 0, step, 0)
        ends = [ends[0] + in_x, ends[1] + (step - in_x)]
    for axis in range(2):
        for slot in range(SLOTS):
            table[LOW + table[SEND_DOWN + axis * LIST + slot]] = ELEMENTS + slot
        end = jnp.int32(SEND_UP + axis * LIST)
        for row in range(ROWS):
            element = user[ROWS * (1 + axis) + row]
            table[end] = element
            end = end + jnp.where(element < 0, 0, 1)
        for slot in range(SLOTS):
            at = table[SEND_UP + axis * LIST + slot] * 4 + axis
            table[UPP + at] = ELEMENTS + slot
            if axis == 0:
                table[ROW_UPP + at] = ROWS + slot
    source_copy.wait()
    into_pairs(source, pairs, 0)
    for slot in range(SLOTS):
        row = table[ROW_LOW + table[SEND_DOWN + slot]]
        down_x[slot] = pairs[pl.ds(pl.multiple_of(row * 8, 8), 8), :]
    for copy in copies:
        copy.wait()


def split_kernel(early, matrix, parts, late, sems):
    copies = matrix_copies(matrix, late, EARLY, ELEMENTS, sems)
    for copy in copies:
        copy.start()

    def split(full, element):
        top = full.astype(jnp.bfloat16)
        parts[element, :ORDER] = top
        parts[element, ORDER:] = (full - top.astype(jnp.float32)).astype(jnp.bfloat16)

    @pl.loop(0, EARLY)
    def _(element):
        split(early[element], element)

    for i, copy in enumerate(copies):
        copy.wait()
        split(late[i], EARLY + i)


def multiply(step, table, get, parts, vector, flux, sends, moments, sums, left):
    low_half = in_low_half((SOURCES, 128))
    norm = jnp.zeros((SOURCES, 128), jnp.float32)
    energy = jnp.zeros((SOURCES, 128), jnp.float32)
    for element in range(ELEMENTS):
        tiles = []
        for axis in range(3):
            tile = get(element, axis)
            tiles.append(tile)
            if vector is not None:
                vector[element, axis] = tile
            norm = norm + tile * tile
            first = tile.astype(jnp.bfloat16)
            rest = tile - first.astype(jnp.float32)
            second = rest.astype(jnp.bfloat16)
            third = (rest - second.astype(jnp.float32)).astype(jnp.bfloat16)
            for part, value in enumerate((first, second, third)):
                for begin in (axis * 128, ORDER + axis * 128):
                    left[element, part * 16 : part * 16 + 16, begin : begin + 128] = value
        for axis in range(3):
            product = jnp.dot(
                left[element],
                parts[element, :, axis * 128 : axis * 128 + 128],
                preferred_element_type=jnp.float32,
            )
            part = product[0:16] + (product[16:32] + product[32:48])
            flux[element, axis] = part
            energy = energy + tiles[axis] * part
    for axis in range(2):
        for slot in range(4):
            at = SEND_UP + axis * LIST + slot
            up = jnp.where(
                low_half, pltpu.roll(flux[table[at + 4], axis], 64, 1), flux[table[at], axis]
            )
            if step == 2:
                sends[axis][slot] = up
                continue
            at = SEND_DOWN + axis * LIST + slot
            down = jnp.where(
                low_half, flux[table[at] >> 2, axis], pltpu.roll(flux[table[at + 4] >> 2, axis], 64, 1)
            )
            odd = table[ODD + axis] == 1
            sends[2 * axis][slot] = jnp.where(odd, down, up)
            sends[2 * axis + 1][slot] = jnp.where(odd, up, down)
    now = with_moments(step, norm, energy, moments)
    if step < 2:
        sums[...] = now
    else:
        sums[...] = jnp.broadcast_to(jnp.sum(now, axis=0, keepdims=True), sums.shape)


def with_moments(step, norm, energy, moments):
    shape = (SOURCES, 128)
    lane = lax.broadcasted_iota(jnp.int32, shape, 1)
    source = lax.broadcasted_iota(jnp.int32, shape, 0)
    half_norm = 0.5 * jnp.sum(norm, axis=1, keepdims=True)
    whole_energy = jnp.sum(energy, axis=1, keepdims=True)
    before = jnp.zeros(shape, jnp.float32) if moments is None else moments[...]
    place = lane - 2 * step * SOURCES - source
    return jnp.where(place == 0, half_norm, jnp.where(place == SOURCES, whole_energy, before))


def tile_of(below, above):
    low_half = in_low_half((8, 128))
    even = jnp.where(low_half, below, pltpu.roll(above, 64, 1))
    odd = jnp.where(low_half, pltpu.roll(below, 64, 1), above)
    return jnp.concatenate([even, odd], axis=0)


def first_kernel(table, pairs, next_y, next_x, parts,
                 flux, xa, xb, ya, yb, sums, rows, left):
    rows[: ROWS * 8, :] = pairs[...]
    for slot in range(SLOTS):
        rows[(ROWS + slot) * 8 : (ROWS + slot) * 8 + 8, :] = next_x[slot]
    into_pairs(next_y, rows, ROWS + SLOTS)

    def face(at):
        return rows[pl.ds(pl.multiple_of(table[at] * 8, 8), 8), :]

    def get(element, axis):
        at = element * 4 + axis
        return tile_of(face(ROW_LOW + at), face(ROW_UPP + at))

    multiply(0, table, get, parts, None, flux, (xa, xb, ya, yb), None, sums, left)


def gather_flux(table, previous, received, every):
    low_half = in_low_half((SOURCES, 128))
    every[0:ELEMENTS] = previous[...]
    for axis in range(2):
        ahead_low = jnp.logical_xor(low_half, table[ODD + axis] == 1)
        for slot in range(4):
            one = received[2 * axis][slot]
            two = received[2 * axis + 1][slot]
            every[ELEMENTS + slot, axis] = jnp.where(ahead_low, one, two)
            every[ELEMENTS + slot + 4, axis] = pltpu.roll(jnp.where(ahead_low, two, one), 64, 1)


def later_kernel(step, table, previous, yb, xa, xb, ya, moments, parts, vector, flux, *rest):
    *sends, sums, every, left = rest
    low_half = in_low_half((SOURCES, 128))
    gather_flux(table, previous, (xa, xb, ya, yb), every)

    def get(element, axis):
        at = element * 4 + axis
        across = jnp.where(low_half, every[table[UPP + at], axis], every[table[LOW + at], axis])
        return every[element, axis] + pltpu.roll(across, 64, 1)

    multiply(step, table, get, parts, vector, flux, sends, moments, sums, left)


def two_sum(a, b):
    total = a + b
    part = total - a
    return total, (a - (total - part)) + (b - part)


def halves(a):
    big = 4097.0 * a
    top = big - (big - a)
    return top, a - top


def two_product(a, b):
    total = a * b
    a1, a2 = halves(a)
    b1, b2 = halves(b)
    return total, ((a1 * b1 - total) + a1 * b2 + a2 * b1) + a2 * b2


def quick(a, b):
    total = a + b
    return total, b - (total - a)


def pair_times(a, b):
    total, rest = two_product(a[0], b[0])
    return quick(total, rest + (a[0] * b[1] + a[1] * b[0]))


def pair_minus(a, b):
    total, rest = two_sum(a[0], -b[0])
    return quick(total, rest + (a[1] - b[1]))


def pair_over(a, b):
    first = a[0] / b[0]
    left = pair_minus(a, pair_times((first, jnp.zeros_like(first)), b))
    return quick(first, left[0] / b[0])


def coefficients(mu):
    centre_0 = pair_over(mu[1], mu[0])
    bent = {i: pair_minus(mu[i + 1], pair_times(centre_0, mu[i])) for i in range(1, 5)}
    slope_1 = pair_over(bent[2], bent[1])
    centre_1 = pair_minus(slope_1, centre_0)
    span_1 = pair_over(bent[1], mu[0])
    twice = {
        i: pair_minus(
            pair_minus(bent[i + 1], pair_times(centre_1, bent[i])), pair_times(span_1, mu[i])
        )
        for i in (2, 3)
    }
    centre_2 = twice[3][0] / twice[2][0] - slope_1[0]
    span_2 = twice[2][0] / bent[1][0]
    alpha_0 = 1.0 / centre_0[0]
    beta_0 = span_1[0] * alpha_0 * alpha_0
    alpha_1 = 1.0 / (centre_1[0] - span_1[0] * alpha_0)
    beta_1 = span_2 * alpha_1 * alpha_1
    alpha_2 = 1.0 / (centre_2 - span_2 * alpha_1)
    return alpha_0, beta_0, alpha_1, beta_1, alpha_2


def total_of(shares):
    parts = [(shares[i : i + 8], jnp.zeros((8, 128), jnp.float32)) for i in range(0, shares.shape[0], 8)]

    def add(a, b):
        total, lost = two_sum(a[0], b[0])
        return total, a[1] + b[1] + lost

    while len(parts) > 1:
        parts = [add(a, b) for a, b in zip(parts[::2], parts[1::2])]
    value = parts[0]
    for shift in (4, 2, 1):
        value = add(value, tuple(pltpu.roll(v, shift, 0) for v in value))
    return value


def final_kernel(table, shares, pairs, firsts, seconds, flux, prev_y, prev_x, answer, residual,
                 every, answer_pairs, residual_pairs):
    low_half = in_low_half((8, 128))
    total = total_of(shares)
    lane = lax.broadcasted_iota(jnp.int32, (8, 128), 1)
    row_of = lax.broadcasted_iota(jnp.int32, (8, 128), 0)

    def packed(tile):
        return jnp.where(low_half, tile[:8], pltpu.roll(tile[8:], 64, 1))

    def moment(part, i):
        even = jnp.sum(jnp.where(lane == i * SOURCES + row_of, total[part], 0.0), axis=1, keepdims=True)
        odd = jnp.sum(jnp.where(lane == i * SOURCES + 8 + row_of, total[part], 0.0), axis=1, keepdims=True)
        return jnp.where(low_half, even, odd)

    mu = [(moment(0, i), moment(1, i)) for i in range(6)]
    alpha_0, beta_0, alpha_1, beta_1, alpha_2 = coefficients(mu)
    every[0:ELEMENTS] = flux[...]
    for axis, prev in enumerate((prev_x, prev_y)):
        for slot in range(4):
            every[ELEMENTS + slot, axis] = prev[slot]
            every[ELEMENTS + slot + 4, axis] = pltpu.roll(prev[slot], 64, 1)
    for element in range(ELEMENTS):
        for axis in range(3):
            at = element * 4 + axis
            row = pl.ds(pl.multiple_of(table[ROW_LOW + at] * 8, 8), 8)
            other = every[table[LOW + at], axis]
            k0 = pairs[row, :]
            k1 = packed(firsts[element, axis])
            k2 = packed(seconds[element, axis])
            k3 = packed(every[element, axis]) + jnp.where(low_half, pltpu.roll(other[:8], 64, 1), other[8:])
            r1 = k0 - alpha_0 * k1
            ar1 = k1 - alpha_0 * k2
            aar1 = k2 - alpha_0 * k3
            d1 = r1 + beta_0 * k0
            ad1 = ar1 + beta_0 * k1
            aad1 = aar1 + beta_0 * k2
            r2 = r1 - alpha_1 * ad1
            ar2 = ar1 - alpha_1 * aad1
            d2 = r2 + beta_1 * d1
            ad2 = ar2 + beta_1 * ad1
            answer_pairs[row, :] = alpha_0 * k0 + (alpha_1 * d1 + alpha_2 * d2)
            residual_pairs[row, :] = r2 - alpha_2 * ad2
    for block, out in ((answer_pairs, answer), (residual_pairs, residual)):
        for group in range(ROWS // 8):
            for pair in range(8):
                out[group * 8 : group * 8 + 8, pair * 128 : pair * 128 + 128] = block[
                    pl.ds(group * 64 + pair, 8, stride=8), :
                ]


def passed(value, axis, target):
    count = lax.axis_size(axis)
    return lax.ppermute(value, axis, [(i, target(i)) for i in range(count)])


def ahead(value, axis):
    return passed(value, axis, lambda i: (i + 1) % lax.axis_size(axis))


def back(value, axis):
    return passed(value, axis, lambda i: (i - 1) % lax.axis_size(axis))


def swapped(value, axis, turn):
    count = lax.axis_size(axis)
    return passed(value, axis, lambda i: (i + 1 - 2 * ((i + turn) % 2)) % count)


def exchanged(sends):
    xa, xb, ya, yb = sends
    yb = swapped(yb, "gy", 1)
    return yb, swapped(xa, "gx", 0), swapped(xb, "gx", 1), swapped(ya, "gy", 0)


def local(heat_source, stiffness, element_faces):
    outer, inner = lax.axis_size("gx"), lax.axis_size("gy")
    pack = vmem((4, SOURCES, 128))
    state = vmem((ELEMENTS, 3, SOURCES, 128))
    matrix = vmem((ELEMENTS, 2 * ORDER, ORDER), jnp.bfloat16)
    moment = vmem((SOURCES, 128))
    left = pltpu.VMEM((ELEMENTS, 48, 2 * ORDER), jnp.bfloat16)
    every = pltpu.VMEM((ELEMENTS + SLOTS, 3, SOURCES, 128), jnp.float32)
    pairs_shape = (ROWS * 8, 128)

    next_y = back(heat_source, "gy")
    table, pairs, down_x, early = pl.pallas_call(
        functools.partial(table_kernel, outer, inner),
        out_shape=(
            pltpu.SMEM((TABLE,), jnp.int32),
            vmem(pairs_shape),
            vmem((SLOTS, 8, 128)),
            vmem((EARLY, ORDER, ORDER)),
        ),
        in_specs=[HBM, HBM, HBM],
        out_specs=(SMEM, VMEM, VMEM, VMEM),
        scratch_shapes=[
            pltpu.SMEM((ROWS,), jnp.int32),
            pltpu.SMEM((3 * ROWS,), jnp.int32),
            pltpu.SMEM((6, ELEMENTS), jnp.int32),
            pltpu.VMEM((ROWS, SOURCES * BLOCK), jnp.float32),
            pltpu.SemaphoreType.DMA((EARLY,)),
            pltpu.SemaphoreType.DMA,
            pltpu.SemaphoreType.DMA,
        ],
        compiler_params=params(52),
        name="table",
    )(element_faces.T, heat_source, stiffness)
    parts = pl.pallas_call(
        split_kernel,
        out_shape=matrix,
        in_specs=[VMEM, HBM],
        out_specs=VMEM,
        scratch_shapes=[
            pltpu.VMEM((ELEMENTS - EARLY, ORDER, ORDER), jnp.float32),
            pltpu.SemaphoreType.DMA((ELEMENTS - EARLY,)),
        ],
        compiler_params=params(34),
        cost_estimate=pl.CostEstimate(flops=10_000_000, bytes_accessed=18 << 20, transcendentals=0),
        name="split",
    )(early, stiffness)
    flux, *sends, moments = pl.pallas_call(
        first_kernel,
        out_shape=(state, pack, pack, pack, pack, moment),
        in_specs=[SMEM] + [VMEM] * 4,
        out_specs=(VMEM,) * 6,
        scratch_shapes=[pltpu.VMEM(((2 * ROWS + SLOTS) * 8, 128), jnp.float32), left],
        compiler_params=params(),
        name="first",
    )(table, pairs, next_y, back(down_x, "gx"), parts)
    k1, flux, *sends, moments = pl.pallas_call(
        functools.partial(later_kernel, 1),
        out_shape=(state, state, pack, pack, pack, pack, moment),
        in_specs=[SMEM] + [VMEM] * 7,
        out_specs=(VMEM,) * 7,
        scratch_shapes=[every, left],
        compiler_params=params(),
        name="second",
    )(table, flux, *exchanged(sends), moments, parts)
    k2, flux, up_x, up_y, shares = pl.pallas_call(
        functools.partial(later_kernel, 2),
        out_shape=(state, state, pack, pack, vmem((outer * inner, 128))),
        in_specs=[SMEM] + [VMEM] * 7,
        out_specs=(VMEM,) * 5,
        scratch_shapes=[every, left],
        compiler_params=params(),
        name="third",
    )(table, flux, *exchanged(sends), moments, parts)
    prev_y, prev_x = ahead(up_y, "gy"), ahead(up_x, "gx")
    shares = lax.all_to_all(shares, ("gx", "gy"), 0, 0, tiled=True)
    natural = jax.ShapeDtypeStruct((ROWS, SOURCES * BLOCK), jnp.float32)
    return pl.pallas_call(
        final_kernel,
        out_shape=(natural, natural),
        in_specs=[SMEM] + [VMEM] * 7,
        out_specs=(VMEM, VMEM),
        scratch_shapes=[every, pltpu.VMEM(pairs_shape, jnp.float32), pltpu.VMEM(pairs_shape, jnp.float32)],
        compiler_params=params(),
        name="final",
    )(table, shares, pairs, k1, k2, flux, prev_y, prev_x)


def solution(mesh):
    return jax.shard_map(
        local,
        mesh=mesh,
        in_specs=(P(("gx", "gy"), None), P(("gx", "gy"), None, None), P(("gx", "gy"), None)),
        out_specs=(P(("gx", "gy"), None), P(("gx", "gy"), None)),
        check_vma=False,
    )
```

```python
import functools

import jax
import jax.numpy as jnp
from jax import lax
from jax.experimental import pallas as pl
from jax.experimental.pallas import tpu as pltpu
from jax.sharding import PartitionSpec as P

BLOCK = 64
SOURCES = 16
ELEMENTS = 16
ROWS = 48
SLOTS = 8
ORDER = 384
EARLY = 6

LOW = 0
UPP = 68
ROW_LOW = 132
ROW_UPP = 196
SEND_UP = 260
SEND_DOWN = 278
LIST = 9
ODD = 296
TABLE = 304

VMEM = pl.BlockSpec(memory_space=pltpu.VMEM)
SMEM = pl.BlockSpec(memory_space=pltpu.SMEM)
HBM = pl.BlockSpec(memory_space=pltpu.HBM)


def params(mebibytes=24):
    return pltpu.CompilerParams(vmem_limit_bytes=mebibytes << 20)


def vmem(shape, dtype=jnp.float32):
    return pltpu.VMEM(shape, dtype)


def in_low_half(shape):
    return lax.broadcasted_iota(jnp.int32, shape, len(shape) - 1) < BLOCK


def into_pairs(source, pairs, first):
    for group in range(ROWS // 8):
        for pair in range(8):
            pairs[pl.ds((first + group * 8) * 8 + pair, 8, stride=8), :] = source[
                group * 8 : group * 8 + 8, pair * 128 : pair * 128 + 128
            ]


def matrix_copies(matrix, target, begin, end, sems):
    return [
        pltpu.make_async_copy(matrix.at[i], target.at[i - begin], sems.at[i - begin])
        for i in range(begin, end)
    ]


def table_kernel(outer, inner, faces_hbm, source_hbm, matrix, table, pairs, down_x, early,
                 owner, user, faces, source, sems, faces_sem, source_sem):
    faces_copy = pltpu.make_async_copy(faces_hbm, faces, faces_sem)
    source_copy = pltpu.make_async_copy(source_hbm, source, source_sem)
    faces_copy.start()
    source_copy.start()
    copies = matrix_copies(matrix, early, 0, EARLY, sems)
    for copy in copies:
        copy.start()
    at_x, at_y = lax.axis_index("gx"), lax.axis_index("gy")
    own = (at_x * inner + at_y) * ROWS
    shifts = (
        (lax.rem(at_x + 1, outer) * inner + at_y) * ROWS - ROWS,
        (at_x * inner + lax.rem(at_y + 1, inner)) * ROWS - 2 * ROWS,
    )
    table[ODD] = lax.rem(at_x, 2)
    table[ODD + 1] = lax.rem(at_y, 2)
    for row in range(3 * ROWS):
        user[row] = -1
    faces_copy.wait()
    for element in range(ELEMENTS):
        for axis in range(3):
            at = element * 4 + axis
            row = faces[2 * axis, element] - own
            owner[row] = at
            table[ROW_LOW + at] = row
            face = faces[2 * axis + 1, element]
            row = face - own
            if axis < 2:
                here = jnp.logical_and(row >= 0, row < ROWS)
                row = jnp.where(here, row, face - shifts[axis])
            user[row] = element
            if axis == 1:
                row = jnp.where(here, row, row - (ROWS - SLOTS))
            table[ROW_UPP + at] = row
    ends = [jnp.int32(SEND_DOWN), jnp.int32(SEND_DOWN + LIST)]
    for row in range(ROWS):
        ref = owner[row]
        axis = ref & 3
        other = user[row]
        table[LOW + ref] = other
        table[UPP + other * 4 + axis] = ref >> 2
        table[jnp.where(axis == 0, ends[0], ends[1])] = ref
        step = jnp.where(other < 0, 1, 0)
        in_x = jnp.where(axis == 0, step, 0)
        ends = [ends[0] + in_x, ends[1] + (step - in_x)]
    for axis in range(2):
        for slot in range(SLOTS):
            table[LOW + table[SEND_DOWN + axis * LIST + slot]] = ELEMENTS + slot
        end = jnp.int32(SEND_UP + axis * LIST)
        for row in range(ROWS):
            element = user[ROWS * (1 + axis) + row]
            table[end] = element
            end = end + jnp.where(element < 0, 0, 1)
        for slot in range(SLOTS):
            at = table[SEND_UP + axis * LIST + slot] * 4 + axis
            table[UPP + at] = ELEMENTS + slot
            if axis == 0:
                table[ROW_UPP + at] = ROWS + slot
    source_copy.wait()
    into_pairs(source, pairs, 0)
    for slot in range(SLOTS):
        row = table[ROW_LOW + table[SEND_DOWN + slot]]
        down_x[slot] = pairs[pl.ds(pl.multiple_of(row * 8, 8), 8), :]
    for copy in copies:
        copy.wait()


def split_kernel(early, matrix, parts, late, sems):
    copies = matrix_copies(matrix, late, EARLY, ELEMENTS, sems)
    for copy in copies:
        copy.start()

    def split(full, element):
        top = full.astype(jnp.bfloat16)
        parts[element, :ORDER] = top
        parts[element, ORDER:] = (full - top.astype(jnp.float32)).astype(jnp.bfloat16)

    @pl.loop(0, EARLY)
    def _(element):
        split(early[element], element)

    for i, copy in enumerate(copies):
        copy.wait()
        split(late[i], EARLY + i)


def multiply(step, table, get, parts, vector, flux, sends, moments, sums, left):
    low_half = in_low_half((SOURCES, 128))
    norm = jnp.zeros((SOURCES, 128), jnp.float32)
    energy = jnp.zeros((SOURCES, 128), jnp.float32)
    for element in range(ELEMENTS):
        tiles = []
        for axis in range(3):
            tile = get(element, axis)
            tiles.append(tile)
            if vector is not None:
                vector[element, axis] = tile
            norm = norm + tile * tile
            first = tile.astype(jnp.bfloat16)
            rest = tile - first.astype(jnp.float32)
            second = rest.astype(jnp.bfloat16)
            third = (rest - second.astype(jnp.float32)).astype(jnp.bfloat16)
            for part, value in enumerate((first, second, third)):
                for begin in (axis * 128, ORDER + axis * 128):
                    left[element, part * 16 : part * 16 + 16, begin : begin + 128] = value
        for axis in range(3):
            product = jnp.dot(
                left[element],
                parts[element, :, axis * 128 : axis * 128 + 128],
                preferred_element_type=jnp.float32,
            )
            part = product[0:16] + (product[16:32] + product[32:48])
            flux[element, axis] = part
            energy = energy + tiles[axis] * part
    for axis in range(2):
        for slot in range(4):
            at = SEND_UP + axis * LIST + slot
            up = jnp.where(
                low_half, pltpu.roll(flux[table[at + 4], axis], 64, 1), flux[table[at], axis]
            )
            if step == 2:
                sends[axis][slot] = up
                continue
            at = SEND_DOWN + axis * LIST + slot
            down = jnp.where(
                low_half, flux[table[at] >> 2, axis], pltpu.roll(flux[table[at + 4] >> 2, axis], 64, 1)
            )
            odd = table[ODD + axis] == 1
            sends[2 * axis][slot] = jnp.where(odd, down, up)
            sends[2 * axis + 1][slot] = jnp.where(odd, up, down)
    now = with_moments(step, norm, energy, moments)
    if step < 2:
        sums[...] = now
    else:
        sums[...] = jnp.broadcast_to(jnp.sum(now, axis=0, keepdims=True), sums.shape)


def with_moments(step, norm, energy, moments):
    shape = (SOURCES, 128)
    lane = lax.broadcasted_iota(jnp.int32, shape, 1)
    source = lax.broadcasted_iota(jnp.int32, shape, 0)
    half_norm = 0.5 * jnp.sum(norm, axis=1, keepdims=True)
    whole_energy = jnp.sum(energy, axis=1, keepdims=True)
    before = jnp.zeros(shape, jnp.float32) if moments is None else moments[...]
    place = lane - 2 * step * SOURCES - source
    return jnp.where(place == 0, half_norm, jnp.where(place == SOURCES, whole_energy, before))


def tile_of(below, above):
    low_half = in_low_half((8, 128))
    even = jnp.where(low_half, below, pltpu.roll(above, 64, 1))
    odd = jnp.where(low_half, pltpu.roll(below, 64, 1), above)
    return jnp.concatenate([even, odd], axis=0)


def first_kernel(table, pairs, next_y, next_x, parts,
                 flux, xa, xb, ya, yb, sums, rows, left):
    rows[: ROWS * 8, :] = pairs[...]
    for slot in range(SLOTS):
        rows[(ROWS + slot) * 8 : (ROWS + slot) * 8 + 8, :] = next_x[slot]
    into_pairs(next_y, rows, ROWS + SLOTS)

    def face(at):
        return rows[pl.ds(pl.multiple_of(table[at] * 8, 8), 8), :]

    def get(element, axis):
        at = element * 4 + axis
        return tile_of(face(ROW_LOW + at), face(ROW_UPP + at))

    multiply(0, table, get, parts, None, flux, (xa, xb, ya, yb), None, sums, left)


def gather_flux(table, previous, received, every):
    low_half = in_low_half((SOURCES, 128))
    every[0:ELEMENTS] = previous[...]
    for axis in range(2):
        ahead_low = jnp.logical_xor(low_half, table[ODD + axis] == 1)
        for slot in range(4):
            one = received[2 * axis][slot]
            two = received[2 * axis + 1][slot]
            every[ELEMENTS + slot, axis] = jnp.where(ahead_low, one, two)
            every[ELEMENTS + slot + 4, axis] = pltpu.roll(jnp.where(ahead_low, two, one), 64, 1)


def later_kernel(step, table, previous, yb, xa, xb, ya, moments, parts, vector, flux, *rest):
    *sends, sums, every, left = rest
    low_half = in_low_half((SOURCES, 128))
    gather_flux(table, previous, (xa, xb, ya, yb), every)

    def get(element, axis):
        at = element * 4 + axis
        across = jnp.where(low_half, every[table[UPP + at], axis], every[table[LOW + at], axis])
        return every[element, axis] + pltpu.roll(across, 64, 1)

    multiply(step, table, get, parts, vector, flux, sends, moments, sums, left)


def two_sum(a, b):
    total = a + b
    part = total - a
    return total, (a - (total - part)) + (b - part)


def halves(a):
    big = 4097.0 * a
    top = big - (big - a)
    return top, a - top


def two_product(a, b):
    total = a * b
    a1, a2 = halves(a)
    b1, b2 = halves(b)
    return total, ((a1 * b1 - total) + a1 * b2 + a2 * b1) + a2 * b2


def quick(a, b):
    total = a + b
    return total, b - (total - a)


def pair_times(a, b):
    total, rest = two_product(a[0], b[0])
    return quick(total, rest + (a[0] * b[1] + a[1] * b[0]))


def pair_minus(a, b):
    total, rest = two_sum(a[0], -b[0])
    return quick(total, rest + (a[1] - b[1]))


def pair_over(a, b):
    first = a[0] / b[0]
    left = pair_minus(a, pair_times((first, jnp.zeros_like(first)), b))
    return quick(first, left[0] / b[0])


def coefficients(mu):
    centre_0 = pair_over(mu[1], mu[0])
    bent = {i: pair_minus(mu[i + 1], pair_times(centre_0, mu[i])) for i in range(1, 5)}
    slope_1 = pair_over(bent[2], bent[1])
    centre_1 = pair_minus(slope_1, centre_0)
    span_1 = pair_over(bent[1], mu[0])
    twice = {
        i: pair_minus(
            pair_minus(bent[i + 1], pair_times(centre_1, bent[i])), pair_times(span_1, mu[i])
        )
        for i in (2, 3)
    }
    centre_2 = twice[3][0] / twice[2][0] - slope_1[0]
    span_2 = twice[2][0] / bent[1][0]
    alpha_0 = 1.0 / centre_0[0]
    beta_0 = span_1[0] * alpha_0 * alpha_0
    alpha_1 = 1.0 / (centre_1[0] - span_1[0] * alpha_0)
    beta_1 = span_2 * alpha_1 * alpha_1
    alpha_2 = 1.0 / (centre_2 - span_2 * alpha_1)
    return alpha_0, beta_0, alpha_1, beta_1, alpha_2


def total_of(shares):
    parts = [(shares[i : i + 8], jnp.zeros((8, 128), jnp.float32)) for i in range(0, shares.shape[0], 8)]

    def add(a, b):
        total, lost = two_sum(a[0], b[0])
        return total, a[1] + b[1] + lost

    while len(parts) > 1:
        parts = [add(a, b) for a, b in zip(parts[::2], parts[1::2])]
    value = parts[0]
    for shift in (4, 2, 1):
        value = add(value, tuple(pltpu.roll(v, shift, 0) for v in value))
    return value


def prepare_kernel(table, pairs, firsts, seconds, flux, prev_y, prev_x, n0, n1, n2, n3,
                   every, *blocks):
    low_half = in_low_half((8, 128))

    def packed(tile):
        return jnp.where(low_half, tile[:8], pltpu.roll(tile[8:], 64, 1))

    every[0:ELEMENTS] = flux[...]
    for axis, prev in enumerate((prev_x, prev_y)):
        for slot in range(4):
            every[ELEMENTS + slot, axis] = prev[slot]
            every[ELEMENTS + slot + 4, axis] = pltpu.roll(prev[slot], 64, 1)
    for element in range(ELEMENTS):
        for axis in range(3):
            at = element * 4 + axis
            row = pl.ds(pl.multiple_of(table[ROW_LOW + at] * 8, 8), 8)
            other = every[table[LOW + at], axis]
            blocks[0][row, :] = packed(firsts[element, axis])
            blocks[1][row, :] = packed(seconds[element, axis])
            blocks[2][row, :] = packed(every[element, axis]) + jnp.where(
                low_half, pltpu.roll(other[:8], 64, 1), other[8:]
            )
    for block, out in zip((pairs, *blocks), (n0, n1, n2, n3)):
        for group in range(ROWS // 8):
            for pair in range(8):
                out[group * 8 : group * 8 + 8, pair * 128 : pair * 128 + 128] = block[
                    pl.ds(group * 64 + pair, 8, stride=8), :
                ]


def final_kernel(shares, n0, n1, n2, n3, answer, residual):
    low_half = in_low_half((8, 128))
    total = total_of(shares)
    lane = lax.broadcasted_iota(jnp.int32, (8, 128), 1)
    row_of = lax.broadcasted_iota(jnp.int32, (8, 128), 0)

    def moment(part, i):
        even = jnp.sum(jnp.where(lane == i * SOURCES + row_of, total[part], 0.0), axis=1, keepdims=True)
        odd = jnp.sum(jnp.where(lane == i * SOURCES + 8 + row_of, total[part], 0.0), axis=1, keepdims=True)
        return jnp.where(low_half, even, odd)

    mu = [(moment(0, i), moment(1, i)) for i in range(6)]
    scalars = coefficients(mu)
    for pair in range(8):
        alpha_0, beta_0, alpha_1, beta_1, alpha_2 = (
            jnp.broadcast_to(v[pair : pair + 1], (8, 128)) for v in scalars
        )
        for group in range(ROWS // 8):
            at = (slice(group * 8, group * 8 + 8), slice(pair * 128, pair * 128 + 128))
            k0, k1, k2, k3 = n0[at], n1[at], n2[at], n3[at]
            r1 = k0 - alpha_0 * k1
            ar1 = k1 - alpha_0 * k2
            aar1 = k2 - alpha_0 * k3
            d1 = r1 + beta_0 * k0
            ad1 = ar1 + beta_0 * k1
            aad1 = aar1 + beta_0 * k2
            r2 = r1 - alpha_1 * ad1
            ar2 = ar1 - alpha_1 * aad1
            d2 = r2 + beta_1 * d1
            ad2 = ar2 + beta_1 * ad1
            answer[at] = alpha_0 * k0 + (alpha_1 * d1 + alpha_2 * d2)
            residual[at] = r2 - alpha_2 * ad2


def passed(value, axis, target):
    count = lax.axis_size(axis)
    return lax.ppermute(value, axis, [(i, target(i)) for i in range(count)])


def ahead(value, axis):
    return passed(value, axis, lambda i: (i + 1) % lax.axis_size(axis))


def back(value, axis):
    return passed(value, axis, lambda i: (i - 1) % lax.axis_size(axis))


def swapped(value, axis, turn):
    count = lax.axis_size(axis)
    return passed(value, axis, lambda i: (i + 1 - 2 * ((i + turn) % 2)) % count)


def exchanged(sends):
    xa, xb, ya, yb = sends
    yb = swapped(yb, "gy", 1)
    return yb, swapped(xa, "gx", 0), swapped(xb, "gx", 1), swapped(ya, "gy", 0)


def local(heat_source, stiffness, element_faces):
    outer, inner = lax.axis_size("gx"), lax.axis_size("gy")
    pack = vmem((4, SOURCES, 128))
    state = vmem((ELEMENTS, 3, SOURCES, 128))
    matrix = vmem((ELEMENTS, 2 * ORDER, ORDER), jnp.bfloat16)
    moment = vmem((SOURCES, 128))
    left = pltpu.VMEM((ELEMENTS, 48, 2 * ORDER), jnp.bfloat16)
    every = pltpu.VMEM((ELEMENTS + SLOTS, 3, SOURCES, 128), jnp.float32)
    pairs_shape = (ROWS * 8, 128)

    next_y = back(heat_source, "gy")
    table, pairs, down_x, early = pl.pallas_call(
        functools.partial(table_kernel, outer, inner),
        out_shape=(
            pltpu.SMEM((TABLE,), jnp.int32),
            vmem(pairs_shape),
            vmem((SLOTS, 8, 128)),
            vmem((EARLY, ORDER, ORDER)),
        ),
        in_specs=[HBM, HBM, HBM],
        out_specs=(SMEM, VMEM, VMEM, VMEM),
        scratch_shapes=[
            pltpu.SMEM((ROWS,), jnp.int32),
            pltpu.SMEM((3 * ROWS,), jnp.int32),
            pltpu.SMEM((6, ELEMENTS), jnp.int32),
            pltpu.VMEM((ROWS, SOURCES * BLOCK), jnp.float32),
            pltpu.SemaphoreType.DMA((EARLY,)),
            pltpu.SemaphoreType.DMA,
            pltpu.SemaphoreType.DMA,
        ],
        compiler_params=params(52),
        name="table",
    )(element_faces.T, heat_source, stiffness)
    parts = pl.pallas_call(
        split_kernel,
        out_shape=matrix,
        in_specs=[VMEM, HBM],
        out_specs=VMEM,
        scratch_shapes=[
            pltpu.VMEM((ELEMENTS - EARLY, ORDER, ORDER), jnp.float32),
            pltpu.SemaphoreType.DMA((ELEMENTS - EARLY,)),
        ],
        compiler_params=params(34),
        cost_estimate=pl.CostEstimate(flops=10_000_000, bytes_accessed=18 << 20, transcendentals=0),
        name="split",
    )(early, stiffness)
    flux, *sends, moments = pl.pallas_call(
        first_kernel,
        out_shape=(state, pack, pack, pack, pack, moment),
        in_specs=[SMEM] + [VMEM] * 4,
        out_specs=(VMEM,) * 6,
        scratch_shapes=[pltpu.VMEM(((2 * ROWS + SLOTS) * 8, 128), jnp.float32), left],
        compiler_params=params(),
        name="first",
    )(table, pairs, next_y, back(down_x, "gx"), parts)
    k1, flux, *sends, moments = pl.pallas_call(
        functools.partial(later_kernel, 1),
        out_shape=(state, state, pack, pack, pack, pack, moment),
        in_specs=[SMEM] + [VMEM] * 7,
        out_specs=(VMEM,) * 7,
        scratch_shapes=[every, left],
        compiler_params=params(),
        name="second",
    )(table, flux, *exchanged(sends), moments, parts)
    k2, flux, up_x, up_y, shares = pl.pallas_call(
        functools.partial(later_kernel, 2),
        out_shape=(state, state, pack, pack, vmem((outer * inner, 128))),
        in_specs=[SMEM] + [VMEM] * 7,
        out_specs=(VMEM,) * 5,
        scratch_shapes=[every, left],
        compiler_params=params(),
        name="third",
    )(table, flux, *exchanged(sends), moments, parts)
    prev_y, prev_x = ahead(up_y, "gy"), ahead(up_x, "gx")
    shares = lax.all_to_all(shares, ("gx", "gy"), 0, 0, tiled=True)
    size = (ROWS, SOURCES * BLOCK)
    natural = jax.ShapeDtypeStruct(size, jnp.float32)
    vectors = pl.pallas_call(
        prepare_kernel,
        out_shape=(vmem(size),) * 4,
        in_specs=[SMEM] + [VMEM] * 6,
        out_specs=(VMEM,) * 4,
        scratch_shapes=[every] + [pltpu.VMEM(pairs_shape, jnp.float32)] * 3,
        compiler_params=params(),
        name="prepare",
    )(table, pairs, k1, k2, flux, prev_y, prev_x)
    return pl.pallas_call(
        final_kernel,
        out_shape=(natural, natural),
        in_specs=[VMEM] * 5,
        out_specs=(VMEM, VMEM),
        compiler_params=params(),
        name="final",
    )(shares, *vectors)


def solution(mesh):
    return jax.shard_map(
        local,
        mesh=mesh,
        in_specs=(P(("gx", "gy"), None), P(("gx", "gy"), None, None), P(("gx", "gy"), None)),
        out_specs=(P(("gx", "gy"), None), P(("gx", "gy"), None)),
        check_vma=False,
    )
```
